512 devices in a mesh: gx: 32 (over y, z_lo), gy: 4 (over z_hi, core), sp: 4 (over x).
Axes of the slice: x: 4, y: 8, z: 8 (z_hi: 2, z_lo: 4; z = z_hi * 4 + z_lo), core: 2. Of those that a mesh axis runs over, the one named last changes fastest.
Arguments:
- latent: float32 [16, 512, 2048], P(None, 'gx', 'gy'), may hold values from -2 to 2
- kappa_sq: float32 [16, 512, 2048], P('sp', 'gx', 'gy'), may hold values from 0.05 to 3
- coefs: float32 [128, 512, 2048], P('sp', 'gx', 'gy'), may hold values from -1.5 to 0.5
- loadings: float32 [128, 16], P('sp'), may hold values from -1.5 to 1.5
- counts: int32 [128, 512, 2048], P('sp', 'gx', 'gy'), may hold values from 0 to 4
- land: int32 [512, 2048], P('gx', 'gy'), may hold values 0 or 1
Outputs:
- grad_latent: float32 [16, 512, 2048], P('sp', 'gx', 'gy')
- grad_loadings: float32 [128, 16], P('sp')
The draws below stay inside these ranges and needn't reach their ends.
All inputs are finite; a program needn't handle non-finite values. No bound on the sum of `land` on one device may be relied on, other than what follows from the above.
Results may differ from the reference program's by a relative error of at most 0.000068.
Values sent between devices are 32-bit elements; how exact they have to be, the bound alone decides.
No kernel may reach another device: no remote copies, remote signals or barrier semaphores. Data moves between devices by JAX's collectives and lax.ppermute only.
A program may use at most 64 MiB of HBM per device.

```python
import math
import jax
import jax.numpy as jnp
from jax import lax

K = 16
S = 128
NX = 512
NY = 2048


def with_ends(entries, own_key, low, largest):
    shape = entries.shape
    place = [jax.random.randint(jax.random.fold_in(own_key, axis), (), 0, shape[axis]) for axis in range(len(shape))]
    entries = entries.at[tuple(place)].set(low)
    longest = shape.index(max(shape))
    place[longest] = (place[longest] + 1) % shape[longest]
    return entries.at[tuple(place)].set(largest)


def steps_of(key, shape, shards, low, high):
    factor_of = 1.0
    for position, shards_of in shards:
        draws = jax.random.uniform(jax.random.fold_in(jax.random.fold_in(key, 6), position), (shards_of,), jnp.float32, low / len(shards), high / len(shards))
        factor_of = factor_of * jnp.repeat(jnp.exp(draws), shape[position] // shards_of).reshape((-1,) + (1,) * (len(shape) - 1 - position))
    return factor_of


def scatter_about(stream_key, shape, scale, reach, pieces=(), held_as=jnp.bfloat16):
    level = steps_of(stream_key, shape, pieces, -0.22, 0.18) if pieces else 1.0
    values = jax.random.normal(stream_key, shape, jnp.float32) * scale * level
    return jnp.minimum(jnp.maximum(values, -reach), reach).astype(held_as)


def setup_inputs(seed: int = 0) -> dict:
    arg_keys = jax.random.split(jax.random.key(seed), 7)
    return {
        "latent": scatter_about(arg_keys[0], (K, NX, NY), 0.3, 2.0, ((1, 32), (2, 4)), jnp.float32),
        "kappa_sq": jnp.clip(jnp.exp(math.log(3.0) - 4.0943445 * jax.random.uniform(arg_keys[1], (K, NX, NY), jnp.float32) ** steps_of(arg_keys[1], (K, NX, NY), ((0, 4), (1, 32), (2, 4)), -0.2, 0.2)), 0.05, 3.0),
        "coefs": jnp.clip(-1.5 + 2.0 * jax.random.uniform(arg_keys[2], (S, NX, NY), jnp.float32) ** steps_of(arg_keys[2], (S, NX, NY), ((0, 4), (1, 32), (2, 4)), -0.2, 0.2), -1.5, 0.5),
        "loadings": scatter_about(arg_keys[3], (S, K), K ** -0.5, 1.5, ((0, 4),), jnp.float32),
        "counts": with_ends(jax.random.randint(arg_keys[4], (S, NX, NY), 0, 5), jax.random.fold_in(arg_keys[4], 1), 0, 4).astype(jnp.int32),
        "land": with_ends((jax.random.randint(arg_keys[5], (NX, NY), 0, 4) < 3).astype(jnp.int32), jax.random.fold_in(arg_keys[5], 1), 0, 1),
    }


def apply_operator(field, kappa):
    padded = jnp.pad(field, ((0, 0), (1, 1), (1, 1)))
    beside = padded[:, 2:, 1:-1] + padded[:, :-2, 1:-1] + padded[:, 1:-1, 2:] + padded[:, 1:-1, :-2]
    return (kappa + 4.0) * field - beside

def reference(latent, kappa_sq, coefs, loadings, counts, land):
    highest = lax.Precision.HIGHEST
    mix = jnp.einsum('sk,kxy->sxy', loadings, latent, precision=highest)
    resid = land.astype(jnp.float32)[None] * (counts.astype(jnp.float32) - jnp.exp(coefs + mix))
    species_part = jnp.einsum('sk,sxy->kxy', loadings, resid, precision=highest)
    prior_part = apply_operator(apply_operator(latent, kappa_sq), kappa_sq)
    grad_latent = species_part - prior_part
    scale = 1.0 / jnp.sqrt(jnp.float32(NX * NY))
    grad_loadings = jnp.einsum('sxy,kxy->sk', resid, latent, precision=highest) * scale
    return (grad_latent, grad_loadings)
```

```python
import functools
import math

import jax
import jax.numpy as jnp
from jax import lax
from jax.experimental import pallas as pl
from jax.experimental.pallas import tpu as pltpu
from jax.sharding import PartitionSpec as P

HIGHEST = lax.Precision.HIGHEST
TILE = 8
LANES = 128


def iota(shape, dim):
    return lax.broadcasted_iota(jnp.int32, shape, dim)


def dot(a, b, contract):
    return lax.dot_general(a, b, (contract, ((), ())), precision=HIGHEST, preferred_element_type=jnp.float32)


def operator(field, kappa, above, below, left, right):
    rows, cols = field.shape
    row, col = iota(field.shape, 0), iota(field.shape, 1)
    up = jnp.where(row == 0, above, pltpu.roll(field, 1, 0))
    down = jnp.where(row == rows - 1, below, pltpu.roll(field, rows - 1, 0))
    west = jnp.where(col == 0, left, pltpu.roll(field, 1, 1))
    east = jnp.where(col == cols - 1, right, pltpu.roll(field, cols - 1, 1))
    return (kappa + 4.0) * field - ((down + up) + (east + west))


def column_to_row(column, offset):
    shape = (column.shape[0], LANES)
    placed = jnp.where(iota(shape, 1) == iota(shape, 0) + offset, column, 0.0)
    return jnp.sum(placed, axis=0, keepdims=True)


def row_to_column(row, count, offset):
    shape = (count, LANES)
    placed = jnp.where(iota(shape, 1) == iota(shape, 0) + offset, row, 0.0)
    return jnp.sum(placed, axis=1, keepdims=True)


def local_kernel(
    steps, peers, across,
    place_ref, loadings_ref, latent_ref, kappa_ref, coefs_ref, counts_ref, land_ref,
    blocks_ref, own_ref, once_ref, head_ref, tail_ref, *rest,
):
    part_refs, (wide_ref, tall_ref, gram_ref, species_ref) = rest[:-4], rest[-4:]
    step = pl.program_id(0)
    fields, species = loadings_ref.shape
    groups = len(part_refs)
    held = fields // groups
    sp, gy = place_ref[0], place_ref[1]
    cols = latent_ref.shape[2]
    flat_fields, flat_species = fields * TILE, species * TILE

    @pl.when(step == 0)
    def _():
        transposed = loadings_ref[...]
        spread = jnp.where(iota((fields, flat_fields), 1) // TILE == iota((fields, flat_fields), 0), 1.0, 0.0)
        wide = dot(transposed, spread, ((0,), (0,)))
        wide = jnp.broadcast_to(wide[:, None, :], (species, TILE, flat_fields)).reshape(flat_species, flat_fields)
        same = iota(wide.shape, 0) % TILE == iota(wide.shape, 1) % TILE
        wide_ref[...] = jnp.where(same, wide, 0.0)
        spread = jnp.where(iota((species, flat_species), 1) // TILE == iota((species, flat_species), 0), 1.0, 0.0)
        tall = dot(transposed, spread, ((1,), (0,)))
        tall = jnp.broadcast_to(tall[:, None, :], (fields, TILE, flat_species)).reshape(flat_fields, flat_species)
        same = iota(tall.shape, 0) % TILE == iota(tall.shape, 1) % TILE
        tall_ref[...] = jnp.where(same, tall, 0.0)

    latent = latent_ref[...].reshape(flat_fields, cols)
    mix = dot(wide_ref[...], latent, ((1,), (0,)))
    rate = jnp.exp(coefs_ref[...].reshape(flat_species, cols) + mix)
    counts = counts_ref[...].reshape(flat_species, cols).astype(jnp.float32)
    land = jnp.broadcast_to(land_ref[...].astype(jnp.float32)[None], (species, TILE, cols))
    resid = land.reshape(flat_species, cols) * (counts - rate)
    gram = dot(resid, latent, ((1,), (1,)))
    species_ref[...] = dot(tall_ref[...], resid, ((1,), (0,))).reshape(fields, TILE, cols)
    at = pl.ds(pl.multiple_of(step * TILE, TILE), TILE)
    for distance, part_ref in enumerate(part_refs):
        owner = lax.rem(sp + distance, groups)
        part_ref[:, at, :] = species_ref[pl.ds(owner * held, held)]
    own_ref[:, at, :] = latent_ref[pl.ds(sp * held, held)]

    @pl.when(step == 0)
    def _():
        gram_ref[...] = gram

    @pl.when(step > 0)
    def _():
        gram_ref[...] += gram

    @pl.when(step == steps - 1)
    def _():
        for k in range(held):
            own = own_ref[k]
            once = operator(own, kappa_ref[k], 0.0, 0.0, 0.0, 0.0)
            once_ref[k] = once
            head_ref[k] = jnp.concatenate([own[:1], once[:1]], axis=0)
            tail_ref[k] = jnp.concatenate([own[-1:], once[-1:]], axis=0)
        total = gram_ref[...]
        same = iota(total.shape, 0) % TILE == iota(total.shape, 1) % TILE
        total = jnp.sum(jnp.where(same, total, 0.0).reshape(species, TILE, flat_fields), axis=1)
        spread = jnp.where(iota((fields, flat_fields), 1) // TILE == iota((fields, flat_fields), 0), 1.0, 0.0)
        total = dot(spread, total, ((1,), (1,)))
        rim = own_ref.shape[1] * held
        west = column_to_row(own_ref[:, :, :1].reshape(rim, 1), 0) + column_to_row(once_ref[:, :, :1].reshape(rim, 1), rim)
        east = column_to_row(own_ref[:, :, cols - 1:].reshape(rim, 1), 0) + column_to_row(once_ref[:, :, cols - 1:].reshape(rim, 1), rim)
        per_row = LANES // species
        sums = fields // per_row
        pieces = [total[q * sums:(q + 1) * sums] for q in range(per_row)]
        packed = jnp.concatenate(pieces, axis=1)
        for peer in range(peers):
            blocks_ref[peer, :sums] = packed[:, None, :]
            blocks_ref[peer, sums] = jnp.where(peer % across < gy, west, east)


def final_kernel(
    scale, down_count, across,
    place_ref, blocks_ref, own_ref, once_ref, kappa_ref, above_ref, below_ref, *rest,
):
    part_refs, (latent_ref, loadings_ref) = rest[:-2], rest[-2:]
    gy, gx = place_ref[1], place_ref[2]
    held, rows, cols = own_ref.shape
    fields, species = loadings_ref.shape
    per_row = LANES // species
    sums = fields // per_row
    for r in range(sums):
        total = jnp.sum(blocks_ref[:, r, :, :], axis=0) * scale
        for q in range(per_row):
            loadings_ref[q * sums + r:q * sums + r + 1, :] = total[:, q * species:(q + 1) * species]

    rim = held * rows
    north, south = jnp.maximum(gx - 1, 0), jnp.minimum(gx + 1, down_count - 1)
    westward, eastward = jnp.maximum(gy - 1, 0), jnp.minimum(gy + 1, across - 1)
    has_north = jnp.where(gx > 0, 1.0, 0.0)
    has_south = jnp.where(gx < down_count - 1, 1.0, 0.0)
    has_west = jnp.where(gy > 0, 1.0, 0.0)
    has_east = jnp.where(gy < across - 1, 1.0, 0.0)

    def halo(i, j):
        return blocks_ref[i * across + j, sums]

    lane = iota((1, LANES), 1)

    def column(j, present):
        middle, upper, lower = halo(gx, j), halo(north, j) * has_north, halo(south, j) * has_south
        first = (lane >= rim) & (lane % rows == 0)
        last = (lane >= rim) & (lane % rows == rows - 1)
        middle = middle - jnp.where(first, pltpu.roll(upper, rim - (rows - 1), 1), 0.0)
        middle = middle - jnp.where(last, pltpu.roll(lower, rim + (rows - 1), 1), 0.0)
        middle = middle * present
        return row_to_column(middle, rim, 0), row_to_column(middle, rim, rim), upper * present, lower * present

    west, west_once, north_west, south_west = column(westward, has_west)
    east, east_once, north_east, south_east = column(eastward, has_east)
    for k in range(held):
        own, kappa = own_ref[k], kappa_ref[k]
        span = slice(k * rows, (k + 1) * rows)
        row, col = iota(own.shape, 0), iota(own.shape, 1)
        once = once_ref[k]
        once = once - jnp.where(row == 0, above_ref[k, :1], 0.0) - jnp.where(row == rows - 1, below_ref[k, :1], 0.0)
        once = once - jnp.where(col == 0, west[span], 0.0) - jnp.where(col == cols - 1, east[span], 0.0)
        edge = iota((1, cols), 1)

        def beside(sent, mine, left, right, at, present):
            corner = k * rows + at
            corners = jnp.where(edge == 0, left[:, corner:corner + 1], 0.0) + jnp.where(edge == cols - 1, right[:, corner:corner + 1], 0.0)
            return (sent - mine - corners) * present

        above = beside(above_ref[k, 1:], own[:1], north_west, north_east, rows - 1, has_north)
        below = beside(below_ref[k, 1:], own[rows - 1:], south_west, south_east, 0, has_south)
        left = (west_once[span] - own[:, :1]) * has_west
        right = (east_once[span] - own[:, cols - 1:]) * has_east
        prior = operator(once, kappa, above, below, left, right)
        species_sum = part_refs[0][k]
        for part_ref in part_refs[1:]:
            species_sum = species_sum + part_ref[k]
        latent_ref[k] = species_sum - prior


def per_device(latent, kappa_sq, coefs, loadings, counts, land):
    fields, rows, cols = latent.shape
    species = loadings.shape[0]
    held = kappa_sq.shape[0]
    down_count, across, groups = lax.axis_size("gx"), lax.axis_size("gy"), lax.axis_size("sp")
    peers = down_count * across
    steps = rows // TILE
    lines = fields * species // LANES + 1
    flat_fields, flat_species = fields * TILE, species * TILE
    f32 = jnp.float32
    place = jnp.stack([lax.axis_index("sp"), lax.axis_index("gy"), lax.axis_index("gx")]).astype(jnp.int32)
    whole = lambda *shape: pl.BlockSpec(shape, lambda t: (0,) * len(shape))
    by_rows = lambda count: pl.BlockSpec((count, TILE, cols), lambda t: (0, t, 0))
    field_block = jax.ShapeDtypeStruct((held, rows, cols), f32)
    edge_block = jax.ShapeDtypeStruct((held, 2, cols), f32)
    smem = pl.BlockSpec(memory_space=pltpu.SMEM)
    blocks, own, once, head, tail, *parts = pl.pallas_call(
        functools.partial(local_kernel, steps, peers, across),
        grid=(steps,),
        in_specs=[
            smem, whole(fields, species), by_rows(fields), whole(held, rows, cols), by_rows(species), by_rows(species),
            pl.BlockSpec((TILE, cols), lambda t: (t, 0)),
        ],
        out_specs=[
            whole(peers, lines, 1, LANES), whole(held, rows, cols), whole(held, rows, cols), whole(held, 2, cols), whole(held, 2, cols),
        ] + [whole(held, rows, cols)] * groups,
        out_shape=[jax.ShapeDtypeStruct((peers, lines, 1, LANES), f32), field_block, field_block, edge_block, edge_block] + [field_block] * groups,
        scratch_shapes=[
            pltpu.VMEM((flat_species, flat_fields), f32),
            pltpu.VMEM((flat_fields, flat_species), f32),
            pltpu.VMEM((flat_species, flat_fields), f32),
            pltpu.VMEM((fields, TILE, cols), f32),
        ],
        compiler_params=pltpu.CompilerParams(vmem_limit_bytes=32 * 2**20),
    )(place, loadings.T, latent, kappa_sq, coefs, counts, land)
    blocks = lax.all_to_all(blocks, ("gx", "gy"), 0, 0, tiled=True)
    arrived = [parts[0]]
    for distance in [2, 1, 3] if groups == 4 else range(1, groups):
        arrived.append(lax.ppermute(parts[distance], "sp", [(i, (i + distance) % groups) for i in range(groups)]))
    above = lax.ppermute(tail, "gx", [(i, i + 1) for i in range(down_count - 1)])
    below = lax.ppermute(head, "gx", [(i + 1, i) for i in range(down_count - 1)])
    vmem = pl.BlockSpec(memory_space=pltpu.VMEM)
    scale = 1.0 / math.sqrt(rows * down_count * cols * across)
    grad_latent, grad_loadings = pl.pallas_call(
        functools.partial(final_kernel, scale, down_count, across),
        in_specs=[smem] + [vmem] * (6 + groups),
        out_specs=[vmem, vmem],
        out_shape=[field_block, jax.ShapeDtypeStruct((fields, species), f32)],
        compiler_params=pltpu.CompilerParams(vmem_limit_bytes=32 * 2**20),
    )(place, blocks, own, once, kappa_sq, above, below, *arrived)
    return grad_latent, grad_loadings.T


def solution(mesh):
    return jax.shard_map(
        per_device,
        mesh=mesh,
        in_specs=(
            P(None, "gx", "gy"),
            P("sp", "gx", "gy"),
            P("sp", "gx", "gy"),
            P("sp", None),
            P("sp", "gx", "gy"),
            P("gx", "gy"),
        ),
        out_specs=(P("sp", "gx", "gy"), P("sp", None)),
        check_vma=False,
    )
```

```python
import functools
import math

import jax
import jax.numpy as jnp
from jax import lax
from jax.experimental import pallas as pl
from jax.experimental.pallas import tpu as pltpu
from jax.sharding import PartitionSpec as P

HIGHEST = lax.Precision.HIGHEST
TILE = 8
LANES = 128
SPLIT = 1


def iota(shape, dim):
    return lax.broadcasted_iota(jnp.int32, shape, dim)


def dot(a, b, contract):
    return lax.dot_general(a, b, (contract, ((), ())), precision=HIGHEST, preferred_element_type=jnp.float32)


def operator(field, kappa, above, below, left, right):
    rows, cols = field.shape
    row, col = iota(field.shape, 0), iota(field.shape, 1)
    up = jnp.where(row == 0, above, pltpu.roll(field, 1, 0))
    down = jnp.where(row == rows - 1, below, pltpu.roll(field, rows - 1, 0))
    west = jnp.where(col == 0, left, pltpu.roll(field, 1, 1))
    east = jnp.where(col == cols - 1, right, pltpu.roll(field, cols - 1, 1))
    return (kappa + 4.0) * field - ((down + up) + (east + west))


def column_to_row(column, offset):
    shape = (column.shape[0], LANES)
    placed = jnp.where(iota(shape, 1) == iota(shape, 0) + offset, column, 0.0)
    return jnp.sum(placed, axis=0, keepdims=True)


def row_to_column(row, count, offset):
    shape = (count, LANES)
    placed = jnp.where(iota(shape, 1) == iota(shape, 0) + offset, row, 0.0)
    return jnp.sum(placed, axis=1, keepdims=True)


def parts_of(value, count):
    parts = []
    for _ in range(count):
        part = value.astype(jnp.bfloat16)
        parts.append(part)
        value = value - part.astype(jnp.float32)
    return parts


def spread_of(rows, cols, dim):
    one, many = iota((rows, cols), dim), iota((rows, cols), 1 - dim)
    return jnp.where(many // TILE == one, 1.0, 0.0)


def on_diagonal(value):
    return jnp.where(iota(value.shape, 0) % TILE == iota(value.shape, 1) % TILE, value, 0.0)


def bf16_dot(a, b, contract):
    return lax.dot_general(a, b, (contract, ((), ())), preferred_element_type=jnp.float32)


def local_kernel(
    peers, across,
    loadings_hbm, latent_hbm, kappa_hbm, coefs_hbm, counts_hbm, land_hbm,
    blocks_ref, own_ref, once_ref, head_ref, tail_ref, *rest,
):
    part_refs, scratch = rest[:-8], rest[-8:]
    (species_ref, loadings_ref, latent_ref, kappa_ref, coefs_ref, counts_ref, land_ref,
     sems) = scratch
    fields, species = loadings_ref.shape
    held, rows, cols = kappa_ref.shape
    sp, gy = lax.axis_index("sp"), lax.axis_index("gy")
    flat_fields, flat_species = fields * TILE, species * TILE
    width = cols // SPLIT
    pieces = [(r, c) for r in range(rows // TILE) for c in range(SPLIT)]
    copies = []
    for n, (r, c) in enumerate(pieces):
        at = (slice(None), pl.ds(r * TILE, TILE), pl.ds(c * width, width))
        pairs = [(latent_hbm, latent_ref), (coefs_hbm, coefs_ref), (counts_hbm, counts_ref)]
        copies.append([
            pltpu.make_async_copy(source.at[at], target.at[at], sems.at[3 * n + i])
            for i, (source, target) in enumerate(pairs)
        ])
    whole = 3 * len(pieces)
    loadings_copy = pltpu.make_async_copy(loadings_hbm, loadings_ref, sems.at[whole])
    land_copy = pltpu.make_async_copy(land_hbm, land_ref, sems.at[whole + 1])
    kappa_copy = pltpu.make_async_copy(kappa_hbm, kappa_ref, sems.at[whole + 2])
    latents = [piece[0] for piece in copies]
    others = [copy for piece in copies for copy in piece[1:]]
    for copy in [loadings_copy, *latents, kappa_copy, land_copy, *others]:
        copy.start()

    loadings_copy.wait()
    transposed = loadings_ref[...]
    wide = dot(transposed, spread_of(fields, flat_fields, 0), ((0,), (0,)))
    wide = jnp.broadcast_to(wide[:, None, :], (species, TILE, flat_fields)).reshape(flat_species, flat_fields)
    wide = parts_of(on_diagonal(wide), 3)
    wide = jnp.concatenate([wide[0], wide[0], wide[0], wide[1], wide[1], wide[2]], axis=1)
    tall = dot(transposed, spread_of(species, flat_species, 0), ((1,), (0,)))
    tall = jnp.broadcast_to(tall[:, None, :], (fields, TILE, flat_species)).reshape(flat_fields, flat_species)
    tall = parts_of(on_diagonal(tall), 2)
    tall = jnp.concatenate([tall[0], tall[0], tall[1]], axis=1)

    spans = [(slice(None), slice(r * TILE, (r + 1) * TILE), slice(c * width, (c + 1) * width)) for r, c in pieces]
    latents, mixes = [], []
    for n, at in enumerate(spans):
        copies[n][0].wait()
        latent = parts_of(latent_ref[at].reshape(flat_fields, width), 3)
        stacked = jnp.concatenate([latent[0], latent[1], latent[2], latent[0], latent[1], latent[0]], axis=0)
        mixes.append(bf16_dot(wide, stacked, ((1,), (0,))))
        latents.append(latent)
    land_copy.wait()
    gram = None
    for n, at in enumerate(spans):
        copies[n][1].wait()
        copies[n][2].wait()
        rate = jnp.exp(coefs_ref[at].reshape(flat_species, width) + mixes[n])
        counts = counts_ref[at].reshape(flat_species, width).astype(jnp.float32)
        land = jnp.broadcast_to(land_ref[at[1:]].astype(jnp.float32)[None], (species, TILE, width))
        resid = parts_of(land.reshape(flat_species, width) * (counts - rate), 2)
        latent = latents[n]
        stacked = jnp.concatenate([resid[0], resid[1], resid[0]], axis=0)
        species_ref[at] = bf16_dot(tall, stacked, ((1,), (0,))).reshape(fields, TILE, width)
        both = bf16_dot(resid[0], jnp.concatenate([latent[0], latent[1]], axis=0), ((1,), (1,)))
        partial = both[:, :flat_fields] + both[:, flat_fields:] + bf16_dot(resid[1], latent[0], ((1,), (1,)))
        gram = partial if gram is None else gram + partial

    kappa_copy.wait()
    first = sp * held
    own_ref[...] = latent_ref[pl.ds(first, held)]
    rim = rows * held
    west, east = jnp.zeros((1, LANES), jnp.float32), jnp.zeros((1, LANES), jnp.float32)
    for k in range(held):
        own = latent_ref[first + k]
        once = operator(own, kappa_ref[k], 0.0, 0.0, 0.0, 0.0)
        once_ref[k] = once
        head_ref[k] = jnp.concatenate([own[:1], once[:1]], axis=0)
        tail_ref[k] = jnp.concatenate([own[-1:], once[-1:]], axis=0)
        west = west + column_to_row(own[:, :1], k * rows) + column_to_row(once[:, :1], rim + k * rows)
        east = east + column_to_row(own[:, cols - 1:], k * rows) + column_to_row(once[:, cols - 1:], rim + k * rows)
    for distance, part_ref in enumerate(part_refs):
        owner = lax.rem(sp + distance, len(part_refs))
        part_ref[...] = species_ref[pl.ds(owner * held, held)]
    total = jnp.sum(on_diagonal(gram).reshape(species, TILE, flat_fields), axis=1)
    total = dot(spread_of(fields, flat_fields, 0), total, ((1,), (1,)))
    per_row = LANES // species
    sums = fields // per_row
    packed = jnp.concatenate([total[q * sums:(q + 1) * sums] for q in range(per_row)], axis=1)
    for peer in range(peers):
        blocks_ref[peer, :sums] = packed[:, None, :]
        blocks_ref[peer, sums] = jnp.where(peer % across < gy, west, east)


def final_kernel(
    scale, down_count, across,
    blocks_ref, own_ref, once_ref, kappa_ref, above_ref, below_ref, *rest,
):
    part_refs, (latent_ref, loadings_ref) = rest[:-2], rest[-2:]
    gy, gx = lax.axis_index("gy"), lax.axis_index("gx")
    held, rows, cols = own_ref.shape
    fields, species = loadings_ref.shape
    per_row = LANES // species
    sums = fields // per_row
    for r in range(sums):
        total = jnp.sum(blocks_ref[:, r, :, :], axis=0) * scale
        for q in range(per_row):
            loadings_ref[q * sums + r:q * sums + r + 1, :] = total[:, q * species:(q + 1) * species]

    rim = held * rows
    north, south = jnp.maximum(gx - 1, 0), jnp.minimum(gx + 1, down_count - 1)
    westward, eastward = jnp.maximum(gy - 1, 0), jnp.minimum(gy + 1, across - 1)
    has_north = jnp.where(gx > 0, 1.0, 0.0)
    has_south = jnp.where(gx < down_count - 1, 1.0, 0.0)
    has_west = jnp.where(gy > 0, 1.0, 0.0)
    has_east = jnp.where(gy < across - 1, 1.0, 0.0)

    def halo(i, j):
        return blocks_ref[i * across + j, sums]

    lane = iota((1, LANES), 1)

    def column(j, present):
        middle, upper, lower = halo(gx, j), halo(north, j) * has_north, halo(south, j) * has_south
        first = (lane >= rim) & (lane % rows == 0)
        last = (lane >= rim) & (lane % rows == rows - 1)
        middle = middle - jnp.where(first, pltpu.roll(upper, rim - (rows - 1), 1), 0.0)
        middle = middle - jnp.where(last, pltpu.roll(lower, rim + (rows - 1), 1), 0.0)
        middle = middle * present
        return row_to_column(middle, rim, 0), row_to_column(middle, rim, rim), upper * present, lower * present

    west, west_once, north_west, south_west = column(westward, has_west)
    east, east_once, north_east, south_east = column(eastward, has_east)
    for k in range(held):
        own, kappa = own_ref[k], kappa_ref[k]
        span = slice(k * rows, (k + 1) * rows)
        row, col = iota(own.shape, 0), iota(own.shape, 1)
        once = once_ref[k]
        once = once - jnp.where(row == 0, above_ref[k, :1], 0.0) - jnp.where(row == rows - 1, below_ref[k, :1], 0.0)
        once = once - jnp.where(col == 0, west[span], 0.0) - jnp.where(col == cols - 1, east[span], 0.0)
        edge = iota((1, cols), 1)

        def beside(sent, mine, left, right, at, present):
            corner = k * rows + at
            corners = jnp.where(edge == 0, left[:, corner:corner + 1], 0.0) + jnp.where(edge == cols - 1, right[:, corner:corner + 1], 0.0)
            return (sent - mine - corners) * present

        above = beside(above_ref[k, 1:], own[:1], north_west, north_east, rows - 1, has_north)
        below = beside(below_ref[k, 1:], own[rows - 1:], south_west, south_east, 0, has_south)
        left = (west_once[span] - own[:, :1]) * has_west
        right = (east_once[span] - own[:, cols - 1:]) * has_east
        prior = operator(once, kappa, above, below, left, right)
        species_sum = part_refs[0][k]
        for part_ref in part_refs[1:]:
            species_sum = species_sum + part_ref[k]
        latent_ref[k] = species_sum - prior


def per_device(latent, kappa_sq, coefs, loadings, counts, land):
    fields, rows, cols = latent.shape
    species = loadings.shape[0]
    held = kappa_sq.shape[0]
    down_count, across, groups = lax.axis_size("gx"), lax.axis_size("gy"), lax.axis_size("sp")
    peers = down_count * across
    lines = fields * species // LANES + 1
    f32 = jnp.float32
    field_block = jax.ShapeDtypeStruct((held, rows, cols), f32)
    edge_block = jax.ShapeDtypeStruct((held, 2, cols), f32)
    vmem = pl.BlockSpec(memory_space=pltpu.VMEM)
    hbm = pl.BlockSpec(memory_space=pltpu.HBM)
    pieces = rows // TILE * SPLIT
    blocks_shape = jax.ShapeDtypeStruct((peers, lines, 1, LANES), f32)
    blocks, own, once, head, tail, *parts = pl.pallas_call(
        functools.partial(local_kernel, peers, across),
        in_specs=[hbm] * 6,
        out_specs=[vmem] * (5 + groups),
        out_shape=[blocks_shape, field_block, field_block, edge_block, edge_block] + [field_block] * groups,
        scratch_shapes=[
            pltpu.VMEM(latent.shape, f32),
            pltpu.VMEM((fields, species), f32),
            pltpu.VMEM(latent.shape, f32),
            pltpu.VMEM(kappa_sq.shape, f32),
            pltpu.VMEM(coefs.shape, f32),
            pltpu.VMEM(counts.shape, jnp.int32),
            pltpu.VMEM(land.shape, jnp.int32),
            pltpu.SemaphoreType.DMA((3 * pieces + 3,)),
        ],
        compiler_params=pltpu.CompilerParams(vmem_limit_bytes=60 * 2**20),
    )(loadings.T, latent, kappa_sq, coefs, counts, land)
    blocks = lax.all_to_all(blocks, ("gx", "gy"), 0, 0, tiled=True)
    arrived = [parts[0]]
    for distance in [2, 1, 3] if groups == 4 else range(1, groups):
        arrived.append(lax.ppermute(parts[distance], "sp", [(i, (i + distance) % groups) for i in range(groups)]))
    above = lax.ppermute(tail, "gx", [(i, i + 1) for i in range(down_count - 1)])
    below = lax.ppermute(head, "gx", [(i + 1, i) for i in range(down_count - 1)])
    scale = 1.0 / math.sqrt(rows * down_count * cols * across)
    grad_latent, grad_loadings = pl.pallas_call(
        functools.partial(final_kernel, scale, down_count, across),
        in_specs=[vmem] * (6 + groups),
        out_specs=[vmem, vmem],
        out_shape=[field_block, jax.ShapeDtypeStruct((fields, species), f32)],
        compiler_params=pltpu.CompilerParams(vmem_limit_bytes=32 * 2**20),
    )(blocks, own, once, kappa_sq, above, below, *arrived)
    return grad_latent, grad_loadings.T


def solution(mesh):
    return jax.shard_map(
        per_device,
        mesh=mesh,
        in_specs=(
            P(None, "gx", "gy"),
            P("sp", "gx", "gy"),
            P("sp", "gx", "gy"),
            P("sp", None),
            P("sp", "gx", "gy"),
            P("gx", "gy"),
        ),
        out_specs=(P("sp", "gx", "gy"), P("sp", None)),
        check_vma=False,
    )
```

```python
import functools
import math

import jax
import jax.numpy as jnp
from jax import lax
from jax.experimental import pallas as pl
from jax.experimental.pallas import tpu as pltpu
from jax.sharding import PartitionSpec as P

HIGHEST = lax.Precision.HIGHEST
TILE = 8
LANES = 128
SPLIT = 1


def iota(shape, dim):
    return lax.broadcasted_iota(jnp.int32, shape, dim)


def dot(a, b, contract):
    return lax.dot_general(a, b, (contract, ((), ())), precision=HIGHEST, preferred_element_type=jnp.float32)


def operator(field, kappa, above, below, left, right):
    rows, cols = field.shape
    row, col = iota(field.shape, 0), iota(field.shape, 1)
    up = jnp.where(row == 0, above, pltpu.roll(field, 1, 0))
    down = jnp.where(row == rows - 1, below, pltpu.roll(field, rows - 1, 0))
    west = jnp.where(col == 0, left, pltpu.roll(field, 1, 1))
    east = jnp.where(col == cols - 1, right, pltpu.roll(field, cols - 1, 1))
    return (kappa + 4.0) * field - ((down + up) + (east + west))


def column_to_row(column, offset):
    shape = (column.shape[0], LANES)
    placed = jnp.where(iota(shape, 1) == iota(shape, 0) + offset, column, 0.0)
    return jnp.sum(placed, axis=0, keepdims=True)


def row_to_column(row, count, offset):
    shape = (count, LANES)
    placed = jnp.where(iota(shape, 1) == iota(shape, 0) + offset, row, 0.0)
    return jnp.sum(placed, axis=1, keepdims=True)


def partner(place, distance, count):
    return place ^ distance if count & (count - 1) == 0 else (place + distance) % count


def parts_of(value, count):
    parts = []
    for _ in range(count):
        part = value.astype(jnp.bfloat16)
        parts.append(part)
        value = value - part.astype(jnp.float32)
    return parts


def spread_of(rows, cols, dim):
    one, many = iota((rows, cols), dim), iota((rows, cols), 1 - dim)
    return jnp.where(many // TILE == one, 1.0, 0.0)


def on_diagonal(value):
    return jnp.where(iota(value.shape, 0) % TILE == iota(value.shape, 1) % TILE, value, 0.0)


def bf16_dot(a, b, contract):
    return lax.dot_general(a, b, (contract, ((), ())), preferred_element_type=jnp.float32)


def local_kernel(
    peers, across,
    loadings_hbm, latent_hbm, kappa_hbm, coefs_hbm, counts_hbm, land_hbm,
    blocks_ref, own_ref, once_ref, odd_ref, even_ref, *rest,
):
    part_refs, scratch = rest[:-8], rest[-8:]
    (species_ref, loadings_ref, latent_ref, kappa_ref, coefs_ref, counts_ref, land_ref,
     sems) = scratch
    fields, species = loadings_ref.shape
    held, rows, cols = kappa_ref.shape
    sp, gy = lax.axis_index("sp"), lax.axis_index("gy")
    flat_fields, flat_species = fields * TILE, species * TILE
    width = cols // SPLIT
    pieces = [(r, c) for r in range(rows // TILE) for c in range(SPLIT)]
    copies = []
    for n, (r, c) in enumerate(pieces):
        at = (slice(None), pl.ds(r * TILE, TILE), pl.ds(c * width, width))
        pairs = [(latent_hbm, latent_ref), (coefs_hbm, coefs_ref), (counts_hbm, counts_ref)]
        copies.append([
            pltpu.make_async_copy(source.at[at], target.at[at], sems.at[3 * n + i])
            for i, (source, target) in enumerate(pairs)
        ])
    whole = 3 * len(pieces)
    loadings_copy = pltpu.make_async_copy(loadings_hbm, loadings_ref, sems.at[whole])
    land_copy = pltpu.make_async_copy(land_hbm, land_ref, sems.at[whole + 1])
    kappa_copy = pltpu.make_async_copy(kappa_hbm, kappa_ref, sems.at[whole + 2])
    latents = [piece[0] for piece in copies]
    others = [copy for piece in copies for copy in piece[1:]]
    for copy in [loadings_copy, *latents, kappa_copy, land_copy, *others]:
        copy.start()

    loadings_copy.wait()
    transposed = loadings_ref[...]
    wide = dot(transposed, spread_of(fields, flat_fields, 0), ((0,), (0,)))
    wide = jnp.broadcast_to(wide[:, None, :], (species, TILE, flat_fields)).reshape(flat_species, flat_fields)
    wide = parts_of(on_diagonal(wide), 3)
    wide = jnp.concatenate([wide[0], wide[0], wide[0], wide[1], wide[1], wide[2]], axis=1)
    tall = dot(transposed, spread_of(species, flat_species, 0), ((1,), (0,)))
    tall = jnp.broadcast_to(tall[:, None, :], (fields, TILE, flat_species)).reshape(flat_fields, flat_species)
    tall = parts_of(on_diagonal(tall), 2)
    tall = jnp.concatenate([tall[0], tall[0], tall[1]], axis=1)

    spans = [(slice(None), slice(r * TILE, (r + 1) * TILE), slice(c * width, (c + 1) * width)) for r, c in pieces]
    latents, mixes = [], []
    for n, at in enumerate(spans):
        copies[n][0].wait()
        latent = parts_of(latent_ref[at].reshape(flat_fields, width), 3)
        stacked = jnp.concatenate([latent[0], latent[1], latent[2], latent[0], latent[1], latent[0]], axis=0)
        mixes.append(bf16_dot(wide, stacked, ((1,), (0,))))
        latents.append(latent)
    land_copy.wait()
    gram = None
    for n, at in enumerate(spans):
        copies[n][1].wait()
        copies[n][2].wait()
        rate = jnp.exp(coefs_ref[at].reshape(flat_species, width) + mixes[n])
        counts = counts_ref[at].reshape(flat_species, width).astype(jnp.float32)
        land = jnp.broadcast_to(land_ref[at[1:]].astype(jnp.float32)[None], (species, TILE, width))
        resid = parts_of(land.reshape(flat_species, width) * (counts - rate), 2)
        latent = latents[n]
        stacked = jnp.concatenate([resid[0], resid[1], resid[0]], axis=0)
        species_ref[at] = bf16_dot(tall, stacked, ((1,), (0,))).reshape(fields, TILE, width)
        both = bf16_dot(resid[0], jnp.concatenate([latent[0], latent[1]], axis=0), ((1,), (1,)))
        partial = both[:, :flat_fields] + both[:, flat_fields:] + bf16_dot(resid[1], latent[0], ((1,), (1,)))
        gram = partial if gram is None else gram + partial

    kappa_copy.wait()
    first = sp * held
    is_even = lax.axis_index("gx") % 2 == 0
    own_ref[...] = latent_ref[pl.ds(first, held)]
    rim = rows * held
    west, east = jnp.zeros((1, LANES), jnp.float32), jnp.zeros((1, LANES), jnp.float32)
    for k in range(held):
        own = latent_ref[first + k]
        once = operator(own, kappa_ref[k], 0.0, 0.0, 0.0, 0.0)
        once_ref[k] = once
        head = jnp.concatenate([own[:1], once[:1]], axis=0)
        tail = jnp.concatenate([own[-1:], once[-1:]], axis=0)
        odd_ref[k] = jnp.where(is_even, head, tail)
        even_ref[k] = jnp.where(is_even, tail, head)
        west = west + column_to_row(own[:, :1], k * rows) + column_to_row(once[:, :1], rim + k * rows)
        east = east + column_to_row(own[:, cols - 1:], k * rows) + column_to_row(once[:, cols - 1:], rim + k * rows)
    for distance, part_ref in enumerate(part_refs):
        owner = partner(sp, distance, len(part_refs))
        part_ref[...] = species_ref[pl.ds(owner * held, held)]
    total = jnp.sum(on_diagonal(gram).reshape(species, TILE, flat_fields), axis=1)
    total = dot(spread_of(fields, flat_fields, 0), total, ((1,), (1,)))
    per_row = LANES // species
    sums = fields // per_row
    packed = jnp.concatenate([total[q * sums:(q + 1) * sums] for q in range(per_row)], axis=1)
    for peer in range(peers):
        blocks_ref[peer, :sums] = packed[:, None, :]
        blocks_ref[peer, sums] = jnp.where(peer % across < gy, west, east)


def final_kernel(
    scale, down_count, across,
    blocks_ref, own_ref, once_ref, kappa_ref, odd_ref, even_ref, *rest,
):
    part_refs, (latent_ref, loadings_ref) = rest[:-2], rest[-2:]
    gy, gx = lax.axis_index("gy"), lax.axis_index("gx")
    held, rows, cols = own_ref.shape
    fields, species = loadings_ref.shape
    per_row = LANES // species
    sums = fields // per_row
    for r in range(sums):
        total = jnp.sum(blocks_ref[:, r, :, :], axis=0) * scale
        for q in range(per_row):
            loadings_ref[q * sums + r:q * sums + r + 1, :] = total[:, q * species:(q + 1) * species]

    rim = held * rows
    is_even = gx % 2 == 0
    north, south = jnp.maximum(gx - 1, 0), jnp.minimum(gx + 1, down_count - 1)
    westward, eastward = jnp.maximum(gy - 1, 0), jnp.minimum(gy + 1, across - 1)
    has_north = jnp.where(gx > 0, 1.0, 0.0)
    has_south = jnp.where(gx < down_count - 1, 1.0, 0.0)
    has_west = jnp.where(gy > 0, 1.0, 0.0)
    has_east = jnp.where(gy < across - 1, 1.0, 0.0)

    def halo(i, j):
        return blocks_ref[i * across + j, sums]

    lane = iota((1, LANES), 1)

    def column(j, present):
        middle, upper, lower = halo(gx, j), halo(north, j) * has_north, halo(south, j) * has_south
        first = (lane >= rim) & (lane % rows == 0)
        last = (lane >= rim) & (lane % rows == rows - 1)
        middle = middle - jnp.where(first, pltpu.roll(upper, rim - (rows - 1), 1), 0.0)
        middle = middle - jnp.where(last, pltpu.roll(lower, rim + (rows - 1), 1), 0.0)
        middle = middle * present
        return row_to_column(middle, rim, 0), row_to_column(middle, rim, rim), upper * present, lower * present

    west, west_once, north_west, south_west = column(westward, has_west)
    east, east_once, north_east, south_east = column(eastward, has_east)
    for k in range(held):
        own, kappa = own_ref[k], kappa_ref[k]
        above_edge = jnp.where(is_even, odd_ref[k], even_ref[k])
        below_edge = jnp.where(is_even, even_ref[k], odd_ref[k])
        span = slice(k * rows, (k + 1) * rows)
        row, col = iota(own.shape, 0), iota(own.shape, 1)
        once = once_ref[k]
        once = once - jnp.where(row == 0, above_edge[:1], 0.0) - jnp.where(row == rows - 1, below_edge[:1], 0.0)
        once = once - jnp.where(col == 0, west[span], 0.0) - jnp.where(col == cols - 1, east[span], 0.0)
        edge = iota((1, cols), 1)

        def beside(sent, mine, left, right, at, present):
            corner = k * rows + at
            corners = jnp.where(edge == 0, left[:, corner:corner + 1], 0.0) + jnp.where(edge == cols - 1, right[:, corner:corner + 1], 0.0)
            return (sent - mine - corners) * present

        above = beside(above_edge[1:], own[:1], north_west, north_east, rows - 1, has_north)
        below = beside(below_edge[1:], own[rows - 1:], south_west, south_east, 0, has_south)
        left = (west_once[span] - own[:, :1]) * has_west
        right = (east_once[span] - own[:, cols - 1:]) * has_east
        prior = operator(once, kappa, above, below, left, right)
        species_sum = part_refs[0][k]
        for part_ref in part_refs[1:]:
            species_sum = species_sum + part_ref[k]
        latent_ref[k] = species_sum - prior


def per_device(latent, kappa_sq, coefs, loadings, counts, land):
    fields, rows, cols = latent.shape
    species = loadings.shape[0]
    held = kappa_sq.shape[0]
    down_count, across, groups = lax.axis_size("gx"), lax.axis_size("gy"), lax.axis_size("sp")
    peers = down_count * across
    lines = fields * species // LANES + 1
    f32 = jnp.float32
    field_block = jax.ShapeDtypeStruct((held, rows, cols), f32)
    edge_block = jax.ShapeDtypeStruct((held, 2, cols), f32)
    vmem = pl.BlockSpec(memory_space=pltpu.VMEM)
    hbm = pl.BlockSpec(memory_space=pltpu.HBM)
    pieces = rows // TILE * SPLIT
    blocks_shape = jax.ShapeDtypeStruct((peers, lines, 1, LANES), f32)
    blocks, own, once, odd_edge, even_edge, *parts = pl.pallas_call(
        functools.partial(local_kernel, peers, across),
        in_specs=[hbm] * 6,
        out_specs=[vmem] * (5 + groups),
        out_shape=[blocks_shape, field_block, field_block, edge_block, edge_block] + [field_block] * groups,
        scratch_shapes=[
            pltpu.VMEM(latent.shape, f32),
            pltpu.VMEM((fields, species), f32),
            pltpu.VMEM(latent.shape, f32),
            pltpu.VMEM(kappa_sq.shape, f32),
            pltpu.VMEM(coefs.shape, f32),
            pltpu.VMEM(counts.shape, jnp.int32),
            pltpu.VMEM(land.shape, jnp.int32),
            pltpu.SemaphoreType.DMA((3 * pieces + 3,)),
        ],
        compiler_params=pltpu.CompilerParams(vmem_limit_bytes=60 * 2**20),
    )(loadings.T, latent, kappa_sq, coefs, counts, land)
    blocks = lax.all_to_all(blocks, ("gx", "gy"), 0, 0, tiled=True)
    arrived = [parts[0]]
    for distance in [2, 1, 3] if groups == 4 else range(1, groups):
        arrived.append(lax.ppermute(parts[distance], "sp", [(i, partner(i, distance, groups)) for i in range(groups)]))

    def exchanged(edge, first):
        pairs = [(i, i + 1) for i in range(first, down_count - 1, 2)]
        return lax.ppermute(edge, "gx", pairs + [(j, i) for i, j in pairs])

    by_odd, by_even = exchanged(odd_edge, 1), exchanged(even_edge, 0)
    scale = 1.0 / math.sqrt(rows * down_count * cols * across)
    grad_latent, grad_loadings = pl.pallas_call(
        functools.partial(final_kernel, scale, down_count, across),
        in_specs=[vmem] * (6 + groups),
        out_specs=[vmem, vmem],
        out_shape=[field_block, jax.ShapeDtypeStruct((fields, species), f32)],
        compiler_params=pltpu.CompilerParams(vmem_limit_bytes=32 * 2**20),
    )(blocks, own, once, kappa_sq, by_odd, by_even, *arrived)
    return grad_latent, grad_loadings.T


def solution(mesh):
    return jax.shard_map(
        per_device,
        mesh=mesh,
        in_specs=(
            P(None, "gx", "gy"),
            P("sp", "gx", "gy"),
            P("sp", "gx", "gy"),
            P("sp", None),
            P("sp", "gx", "gy"),
            P("gx", "gy"),
        ),
        out_specs=(P("sp", "gx", "gy"), P("sp", None)),
        check_vma=False,
    )
```

```python
import functools
import math

import jax
import jax.numpy as jnp
from jax import lax
from jax.experimental import pallas as pl
from jax.experimental.pallas import tpu as pltpu
from jax.sharding import PartitionSpec as P

HIGHEST = lax.Precision.HIGHEST
TILE = 8
LANES = 128
SPLIT = 1
NEAR, FAR = 1, 3


def iota(shape, dim):
    return lax.broadcasted_iota(jnp.int32, shape, dim)


def dot(a, b, contract):
    return lax.dot_general(a, b, (contract, ((), ())), precision=HIGHEST, preferred_element_type=jnp.float32)


def operator(field, kappa, above, below, left, right):
    rows, cols = field.shape
    row, col = iota(field.shape, 0), iota(field.shape, 1)
    up = jnp.where(row == 0, above, pltpu.roll(field, 1, 0))
    down = jnp.where(row == rows - 1, below, pltpu.roll(field, rows - 1, 0))
    west = jnp.where(col == 0, left, pltpu.roll(field, 1, 1))
    east = jnp.where(col == cols - 1, right, pltpu.roll(field, cols - 1, 1))
    return (kappa + 4.0) * field - ((down + up) + (east + west))


def column_to_row(column, offset):
    shape = (column.shape[0], LANES)
    placed = jnp.where(iota(shape, 1) == iota(shape, 0) + offset, column, 0.0)
    return jnp.sum(placed, axis=0, keepdims=True)


def row_to_column(row, count, offset):
    shape = (count, LANES)
    placed = jnp.where(iota(shape, 1) == iota(shape, 0) + offset, row, 0.0)
    return jnp.sum(placed, axis=1, keepdims=True)


def parts_of(value, count):
    parts = []
    for _ in range(count):
        part = value.astype(jnp.bfloat16)
        parts.append(part)
        value = value - part.astype(jnp.float32)
    return parts


def spread_of(rows, cols, dim):
    one, many = iota((rows, cols), dim), iota((rows, cols), 1 - dim)
    return jnp.where(many // TILE == one, 1.0, 0.0)


def on_diagonal(value):
    return jnp.where(iota(value.shape, 0) % TILE == iota(value.shape, 1) % TILE, value, 0.0)


def bf16_dot(a, b, contract):
    return lax.dot_general(a, b, (contract, ((), ())), preferred_element_type=jnp.float32)


def local_kernel(
    peers, across,
    loadings_hbm, latent_hbm, kappa_hbm, coefs_hbm, counts_hbm, land_hbm,
    blocks_ref, own_ref, odd_ref, even_ref, sent_ref, kept_ref,
    species_ref, loadings_ref, latent_ref, kappa_ref, coefs_ref, counts_ref, land_ref, sems,
):
    fields, species = loadings_ref.shape
    held, rows, cols = kappa_ref.shape
    sp, gy = lax.axis_index("sp"), lax.axis_index("gy")
    flat_fields, flat_species = fields * TILE, species * TILE
    width = cols // SPLIT
    pieces = [(r, c) for r in range(rows // TILE) for c in range(SPLIT)]
    copies = []
    for n, (r, c) in enumerate(pieces):
        at = (slice(None), pl.ds(r * TILE, TILE), pl.ds(c * width, width))
        pairs = [(latent_hbm, latent_ref), (coefs_hbm, coefs_ref), (counts_hbm, counts_ref)]
        copies.append([
            pltpu.make_async_copy(source.at[at], target.at[at], sems.at[3 * n + i])
            for i, (source, target) in enumerate(pairs)
        ])
    whole = 3 * len(pieces)
    loadings_copy = pltpu.make_async_copy(loadings_hbm, loadings_ref, sems.at[whole])
    land_copy = pltpu.make_async_copy(land_hbm, land_ref, sems.at[whole + 1])
    kappa_copy = pltpu.make_async_copy(kappa_hbm, kappa_ref, sems.at[whole + 2])
    latents = [piece[0] for piece in copies]
    others = [copy for piece in copies for copy in piece[1:]]
    for copy in [loadings_copy, *latents, kappa_copy, land_copy, *others]:
        copy.start()

    loadings_copy.wait()
    transposed = loadings_ref[...]
    wide = dot(transposed, spread_of(fields, flat_fields, 0), ((0,), (0,)))
    wide = jnp.broadcast_to(wide[:, None, :], (species, TILE, flat_fields)).reshape(flat_species, flat_fields)
    wide = parts_of(on_diagonal(wide), 3)
    wide = jnp.concatenate([wide[0], wide[0], wide[0], wide[1], wide[1], wide[2]], axis=1)
    tall = dot(transposed, spread_of(species, flat_species, 0), ((1,), (0,)))
    tall = jnp.broadcast_to(tall[:, None, :], (fields, TILE, flat_species)).reshape(flat_fields, flat_species)
    tall = parts_of(on_diagonal(tall), 2)
    tall = jnp.concatenate([tall[0], tall[0], tall[1]], axis=1)

    spans = [(slice(None), slice(r * TILE, (r + 1) * TILE), slice(c * width, (c + 1) * width)) for r, c in pieces]
    latents, mixes = [], []
    for n, at in enumerate(spans):
        copies[n][0].wait()
        latent = parts_of(latent_ref[at].reshape(flat_fields, width), 3)
        stacked = jnp.concatenate([latent[0], latent[1], latent[2], latent[0], latent[1], latent[0]], axis=0)
        mixes.append(bf16_dot(wide, stacked, ((1,), (0,))))
        latents.append(latent)
    land_copy.wait()
    gram = None
    for n, at in enumerate(spans):
        copies[n][1].wait()
        copies[n][2].wait()
        rate = jnp.exp(coefs_ref[at].reshape(flat_species, width) + mixes[n])
        counts = counts_ref[at].reshape(flat_species, width).astype(jnp.float32)
        land = jnp.broadcast_to(land_ref[at[1:]].astype(jnp.float32)[None], (species, TILE, width))
        resid = parts_of(land.reshape(flat_species, width) * (counts - rate), 2)
        latent = latents[n]
        stacked = jnp.concatenate([resid[0], resid[1], resid[0]], axis=0)
        species_ref[at] = bf16_dot(tall, stacked, ((1,), (0,))).reshape(fields, TILE, width)
        both = bf16_dot(resid[0], jnp.concatenate([latent[0], latent[1]], axis=0), ((1,), (1,)))
        partial = both[:, :flat_fields] + both[:, flat_fields:] + bf16_dot(resid[1], latent[0], ((1,), (1,)))
        gram = partial if gram is None else gram + partial

    kappa_copy.wait()
    first = sp * held
    is_even = lax.axis_index("gx") % 2 == 0
    own_ref[...] = latent_ref[pl.ds(first, held)]
    rim = rows * held
    west, east = jnp.zeros((1, LANES), jnp.float32), jnp.zeros((1, LANES), jnp.float32)
    for k in range(held):
        own = latent_ref[first + k]
        once = operator(own, kappa_ref[k], 0.0, 0.0, 0.0, 0.0)
        head = jnp.concatenate([own[:1], once[:1]], axis=0)
        tail = jnp.concatenate([own[-1:], once[-1:]], axis=0)
        odd_ref[k] = jnp.where(is_even, head, tail)
        even_ref[k] = jnp.where(is_even, tail, head)
        west = west + column_to_row(own[:, :1], k * rows) + column_to_row(once[:, :1], rim + k * rows)
        east = east + column_to_row(own[:, cols - 1:], k * rows) + column_to_row(once[:, cols - 1:], rim + k * rows)
    for ref, owners in ((kept_ref, (sp, sp ^ FAR)), (sent_ref, (sp ^ NEAR, sp ^ NEAR ^ FAR))):
        for half, owner in enumerate(owners):
            ref[half] = species_ref[pl.ds(owner * held, held)]
    total = jnp.sum(on_diagonal(gram).reshape(species, TILE, flat_fields), axis=1)
    total = dot(spread_of(fields, flat_fields, 0), total, ((1,), (1,)))
    per_row = LANES // species
    sums = fields // per_row
    packed = jnp.concatenate([total[q * sums:(q + 1) * sums] for q in range(per_row)], axis=1)
    for peer in range(peers):
        blocks_ref[peer, :sums] = packed[:, None, :]
        blocks_ref[peer, sums] = jnp.where(peer % across < gy, west, east)


def add_kernel(kept_ref, received_ref, mine_ref, sent_ref):
    mine_ref[...] = kept_ref[0] + received_ref[0]
    sent_ref[...] = kept_ref[1] + received_ref[1]


def prior_kernel(down_count, own_ref, kappa_ref, odd_ref, even_ref, prior_ref):
    gx = lax.axis_index("gx")
    held, rows, cols = own_ref.shape
    is_even = gx % 2 == 0
    has_north = jnp.where(gx > 0, 1.0, 0.0)
    has_south = jnp.where(gx < down_count - 1, 1.0, 0.0)
    for k in range(held):
        own, kappa = own_ref[k], kappa_ref[k]
        above_edge = jnp.where(is_even, odd_ref[k], even_ref[k])
        below_edge = jnp.where(is_even, even_ref[k], odd_ref[k])
        once = operator(own, kappa, above_edge[:1], below_edge[:1], 0.0, 0.0)
        above = (above_edge[1:] - own[:1]) * has_north
        below = (below_edge[1:] - own[rows - 1:]) * has_south
        prior_ref[k] = operator(once, kappa, above, below, 0.0, 0.0)


def final_kernel(scale, down_count, across, blocks_ref, own_ref, kappa_ref, prior_ref, mine_ref, other_ref, latent_ref, loadings_ref):
    gy, gx = lax.axis_index("gy"), lax.axis_index("gx")
    held, rows, cols = own_ref.shape
    fields, species = loadings_ref.shape
    per_row = LANES // species
    sums = fields // per_row
    for r in range(sums):
        total = jnp.sum(blocks_ref[:, r, :, :], axis=0) * scale
        for q in range(per_row):
            loadings_ref[q * sums + r:q * sums + r + 1, :] = total[:, q * species:(q + 1) * species]

    rim = held * rows
    north, south = jnp.maximum(gx - 1, 0), jnp.minimum(gx + 1, down_count - 1)
    has_north = jnp.where(gx > 0, 1.0, 0.0)
    has_south = jnp.where(gx < down_count - 1, 1.0, 0.0)
    lane = iota((1, LANES), 1)

    def column(j, present):
        middle, upper, lower = blocks_ref[gx * across + j, sums], blocks_ref[north * across + j, sums], blocks_ref[south * across + j, sums]
        first, last = lane % rows == 0, lane % rows == rows - 1
        corners = jnp.where(first, pltpu.roll(upper, LANES - (rows - 1), 1), 0.0) * has_north
        corners = corners + jnp.where(last, pltpu.roll(lower, rows - 1, 1), 0.0) * has_south
        corners = jnp.where(lane < rim, corners, 0.0)
        once = pltpu.roll(middle, LANES - rim, 1) - corners
        return [row_to_column(row * present, rim, 0) for row in (middle, once, corners)]

    west = column(jnp.maximum(gy - 1, 0), jnp.where(gy > 0, 1.0, 0.0))
    east = column(jnp.minimum(gy + 1, across - 1), jnp.where(gy < across - 1, 1.0, 0.0))
    row, col = iota((rows, LANES), 0), iota((rows, LANES), 1)

    def addition(k, columns, at, own, kappa, edge, inner, present):
        field, once, corners = [value[k * rows:(k + 1) * rows] for value in columns]
        once = once - own * present
        field = jnp.broadcast_to(field, (rows, LANES))
        beside = jnp.where(row == 0, 0.0, pltpu.roll(field, 1, 0)) + jnp.where(row == rows - 1, 0.0, pltpu.roll(field, rows - 1, 0))
        outer = beside - (kappa + 4.0) * field - once + corners
        return jnp.where(col == edge, outer, 0.0) + jnp.where(col == inner, field, 0.0)

    for k in range(held):
        latent_ref[k] = mine_ref[k] + other_ref[k] - prior_ref[k]
        span = slice(0, LANES)
        latent_ref[k, :, span] -= addition(
            k, west, span, own_ref[k, :, :1], kappa_ref[k, :, span], 0, 1, jnp.where(gy > 0, 1.0, 0.0))
        span = slice(cols - LANES, cols)
        latent_ref[k, :, span] -= addition(
            k, east, span, own_ref[k, :, cols - 1:], kappa_ref[k, :, span], LANES - 1, LANES - 2, jnp.where(gy < across - 1, 1.0, 0.0))


def per_device(latent, kappa_sq, coefs, loadings, counts, land):
    fields, rows, cols = latent.shape
    species = loadings.shape[0]
    held = kappa_sq.shape[0]
    down_count, across, groups = lax.axis_size("gx"), lax.axis_size("gy"), lax.axis_size("sp")
    peers = down_count * across
    lines = fields * species // LANES + 1
    f32 = jnp.float32
    field_block = jax.ShapeDtypeStruct((held, rows, cols), f32)
    edge_block = jax.ShapeDtypeStruct((held, 2, cols), f32)
    vmem = pl.BlockSpec(memory_space=pltpu.VMEM)
    hbm = pl.BlockSpec(memory_space=pltpu.HBM)
    pieces = rows // TILE * SPLIT
    half_block = jax.ShapeDtypeStruct((groups // 2, held, rows, cols), f32)
    blocks, own, odd_edge, even_edge, sent, kept = pl.pallas_call(
        functools.partial(local_kernel, peers, across),
        in_specs=[hbm] * 6,
        out_specs=[vmem] * 6,
        out_shape=[
            jax.ShapeDtypeStruct((peers, lines, 1, LANES), f32), field_block, edge_block, edge_block, half_block, half_block,
        ],
        scratch_shapes=[
            pltpu.VMEM(latent.shape, f32),
            pltpu.VMEM((fields, species), f32),
            pltpu.VMEM(latent.shape, f32),
            pltpu.VMEM(kappa_sq.shape, f32),
            pltpu.VMEM(coefs.shape, f32),
            pltpu.VMEM(counts.shape, jnp.int32),
            pltpu.VMEM(land.shape, jnp.int32),
            pltpu.SemaphoreType.DMA((3 * pieces + 3,)),
        ],
        compiler_params=pltpu.CompilerParams(vmem_limit_bytes=60 * 2**20),
    )(loadings.T, latent, kappa_sq, coefs, counts, land)
    blocks = lax.all_to_all(blocks, ("gx", "gy"), 0, 0, tiled=True)

    def exchanged(edge, first):
        pairs = [(i, i + 1) for i in range(first, down_count - 1, 2)]
        return lax.ppermute(edge, "gx", pairs + [(j, i) for i, j in pairs])

    by_odd, by_even = exchanged(odd_edge, 1), exchanged(even_edge, 0)
    params = pltpu.CompilerParams(vmem_limit_bytes=16 * 2**20)
    received = lax.ppermute(sent, "sp", [(i, i ^ NEAR) for i in range(groups)])
    mine, sent = pl.pallas_call(
        add_kernel,
        in_specs=[vmem] * 2,
        out_specs=[vmem] * 2,
        out_shape=[field_block] * 2,
        compiler_params=params,
        cost_estimate=pl.CostEstimate(flops=10**6, bytes_accessed=2**20, transcendentals=0),
    )(kept, received)
    other = lax.ppermute(sent, "sp", [(i, i ^ FAR) for i in range(groups)])
    prior = pl.pallas_call(
        functools.partial(prior_kernel, down_count),
        in_specs=[vmem] * 4,
        out_specs=vmem,
        out_shape=field_block,
        compiler_params=params,
        cost_estimate=pl.CostEstimate(flops=3*10**9, bytes_accessed=2**20, transcendentals=0),
    )(own, kappa_sq, by_odd, by_even)
    scale = 1.0 / math.sqrt(rows * down_count * cols * across)
    grad_latent, grad_loadings = pl.pallas_call(
        functools.partial(final_kernel, scale, down_count, across),
        in_specs=[vmem] * 6,
        out_specs=[vmem, vmem],
        out_shape=[field_block, jax.ShapeDtypeStruct((fields, species), f32)],
        compiler_params=params,
    )(blocks, own, kappa_sq, prior, mine, other)
    return grad_latent, grad_loadings.T


def solution(mesh):
    return jax.shard_map(
        per_device,
        mesh=mesh,
        in_specs=(
            P(None, "gx", "gy"),
            P("sp", "gx", "gy"),
            P("sp", "gx", "gy"),
            P("sp", None),
            P("sp", "gx", "gy"),
            P("gx", "gy"),
        ),
        out_specs=(P("sp", "gx", "gy"), P("sp", None)),
        check_vma=False,
    )
```

```python
import functools
import math

import jax
import jax.numpy as jnp
from jax import lax
from jax.experimental import pallas as pl
from jax.experimental.pallas import tpu as pltpu
from jax.sharding import PartitionSpec as P

HIGHEST = lax.Precision.HIGHEST
TILE = 8
LANES = 128
SPLIT = 1
NEAR, FAR = 1, 3


def iota(shape, dim):
    return lax.broadcasted_iota(jnp.int32, shape, dim)


def dot(a, b, contract):
    return lax.dot_general(a, b, (contract, ((), ())), precision=HIGHEST, preferred_element_type=jnp.float32)


def operator(field, kappa, above, below, left, right):
    rows, cols = field.shape
    row, col = iota(field.shape, 0), iota(field.shape, 1)
    up = jnp.where(row == 0, above, pltpu.roll(field, 1, 0))
    down = jnp.where(row == rows - 1, below, pltpu.roll(field, rows - 1, 0))
    west = jnp.where(col == 0, left, pltpu.roll(field, 1, 1))
    east = jnp.where(col == cols - 1, right, pltpu.roll(field, cols - 1, 1))
    return (kappa + 4.0) * field - ((down + up) + (east + west))


def column_to_row(column, offset):
    shape = (column.shape[0], LANES)
    placed = jnp.where(iota(shape, 1) == iota(shape, 0) + offset, column, 0.0)
    return jnp.sum(placed, axis=0, keepdims=True)


def row_to_column(row, count, offset):
    shape = (count, LANES)
    placed = jnp.where(iota(shape, 1) == iota(shape, 0) + offset, row, 0.0)
    return jnp.sum(placed, axis=1, keepdims=True)


def parts_of(value, count):
    parts = []
    for _ in range(count):
        part = value.astype(jnp.bfloat16)
        parts.append(part)
        value = value - part.astype(jnp.float32)
    return parts


def spread_of(rows, cols, dim):
    one, many = iota((rows, cols), dim), iota((rows, cols), 1 - dim)
    return jnp.where(many // TILE == one, 1.0, 0.0)


def on_diagonal(value):
    return jnp.where(iota(value.shape, 0) % TILE == iota(value.shape, 1) % TILE, value, 0.0)


def bf16_dot(a, b, contract):
    return lax.dot_general(a, b, (contract, ((), ())), preferred_element_type=jnp.float32)


def local_kernel(
    peers, across,
    loadings_hbm, latent_hbm, kappa_hbm, coefs_hbm, counts_hbm, land_hbm,
    blocks_ref, own_ref, odd_ref, even_ref, sent_ref, kept_ref,
    species_ref, loadings_ref, latent_ref, kappa_ref, coefs_ref, counts_ref, land_ref, sems,
):
    fields, species = loadings_ref.shape
    held, rows, cols = kappa_ref.shape
    sp, gy = lax.axis_index("sp"), lax.axis_index("gy")
    flat_fields, flat_species = fields * TILE, species * TILE
    width = cols // SPLIT
    pieces = [(r, c) for r in range(rows // TILE) for c in range(SPLIT)]
    copies = []
    for n, (r, c) in enumerate(pieces):
        at = (slice(None), pl.ds(r * TILE, TILE), pl.ds(c * width, width))
        pairs = [(latent_hbm, latent_ref), (coefs_hbm, coefs_ref), (counts_hbm, counts_ref)]
        copies.append([
            pltpu.make_async_copy(source.at[at], target.at[at], sems.at[3 * n + i])
            for i, (source, target) in enumerate(pairs)
        ])
    whole = 3 * len(pieces)
    loadings_copy = pltpu.make_async_copy(loadings_hbm, loadings_ref, sems.at[whole])
    land_copy = pltpu.make_async_copy(land_hbm, land_ref, sems.at[whole + 1])
    kappa_copy = pltpu.make_async_copy(kappa_hbm, kappa_ref, sems.at[whole + 2])
    latents = [piece[0] for piece in copies]
    others = [copy for piece in copies for copy in piece[1:]]
    for copy in [loadings_copy, *latents, kappa_copy, land_copy, *others]:
        copy.start()

    loadings_copy.wait()
    transposed = loadings_ref[...]
    wide = dot(transposed, spread_of(fields, flat_fields, 0), ((0,), (0,)))
    wide = jnp.broadcast_to(wide[:, None, :], (species, TILE, flat_fields)).reshape(flat_species, flat_fields)
    wide = parts_of(on_diagonal(wide), 3)
    wide = jnp.concatenate([wide[0], wide[0], wide[0], wide[1], wide[1], wide[2]], axis=1)
    tall = dot(transposed, spread_of(species, flat_species, 0), ((1,), (0,)))
    tall = jnp.broadcast_to(tall[:, None, :], (fields, TILE, flat_species)).reshape(flat_fields, flat_species)
    tall = parts_of(on_diagonal(tall), 2)
    tall = jnp.concatenate([tall[0], tall[0], tall[1]], axis=1)

    spans = [(slice(None), slice(r * TILE, (r + 1) * TILE), slice(c * width, (c + 1) * width)) for r, c in pieces]
    latents, mixes = [], []
    for n, at in enumerate(spans):
        copies[n][0].wait()
        latent = parts_of(latent_ref[at].reshape(flat_fields, width), 3)
        stacked = jnp.concatenate([latent[0], latent[1], latent[2], latent[0], latent[1], latent[0]], axis=0)
        mixes.append(bf16_dot(wide, stacked, ((1,), (0,))))
        latents.append(latent)
    land_copy.wait()
    gram = None
    for n, at in enumerate(spans):
        copies[n][1].wait()
        copies[n][2].wait()
        rate = jnp.exp(coefs_ref[at].reshape(flat_species, width) + mixes[n])
        counts = counts_ref[at].reshape(flat_species, width).astype(jnp.float32)
        land = jnp.broadcast_to(land_ref[at[1:]].astype(jnp.float32)[None], (species, TILE, width))
        resid = parts_of(land.reshape(flat_species, width) * (counts - rate), 2)
        latent = latents[n]
        both = bf16_dot(resid[0], jnp.concatenate([latent[0], latent[1]], axis=0), ((1,), (1,)))
        partial = both[:, :flat_fields] + both[:, flat_fields:] + bf16_dot(resid[1], latent[0], ((1,), (1,)))
        gram = partial if gram is None else gram + partial
        stacked = jnp.concatenate([resid[0], resid[1], resid[0]], axis=0)
        species_ref[at] = bf16_dot(tall, stacked, ((1,), (0,))).reshape(fields, TILE, width)

    kappa_copy.wait()
    first = sp * held
    is_even = lax.axis_index("gx") % 2 == 0
    own_ref[...] = latent_ref[pl.ds(first, held)]
    rim = rows * held
    west, east = jnp.zeros((1, LANES), jnp.float32), jnp.zeros((1, LANES), jnp.float32)
    for k in range(held):
        own = latent_ref[first + k]
        once = operator(own, kappa_ref[k], 0.0, 0.0, 0.0, 0.0)
        head = jnp.concatenate([own[:1], once[:1]], axis=0)
        tail = jnp.concatenate([own[-1:], once[-1:]], axis=0)
        odd_ref[k] = jnp.where(is_even, head, tail)
        even_ref[k] = jnp.where(is_even, tail, head)
        west = west + column_to_row(own[:, :1], k * rows) + column_to_row(once[:, :1], rim + k * rows)
        east = east + column_to_row(own[:, cols - 1:], k * rows) + column_to_row(once[:, cols - 1:], rim + k * rows)
    for ref, owners in ((kept_ref, (sp, sp ^ FAR)), (sent_ref, (sp ^ NEAR, sp ^ NEAR ^ FAR))):
        for half, owner in enumerate(owners):
            ref[half] = species_ref[pl.ds(owner * held, held)]
    total = jnp.sum(on_diagonal(gram).reshape(species, TILE, flat_fields), axis=1)
    total = dot(spread_of(fields, flat_fields, 0), total, ((1,), (1,)))
    per_row = LANES // species
    sums = fields // per_row
    packed = jnp.concatenate([total[q * sums:(q + 1) * sums] for q in range(per_row)], axis=1)
    for peer in range(peers):
        blocks_ref[peer, :sums] = packed[:, None, :]
        blocks_ref[peer, sums] = jnp.where(peer % across < gy, west, east)


def add_kernel(kept_ref, received_ref, mine_ref, sent_ref):
    mine_ref[...] = kept_ref[0] + received_ref[0]
    sent_ref[...] = kept_ref[1] + received_ref[1]


def prior_kernel(
    scale, down_count, across, blocks_ref, own_ref, kappa_ref, mine_ref, odd_ref, even_ref, rest_ref, loadings_ref,
):
    gy, gx = lax.axis_index("gy"), lax.axis_index("gx")
    is_even = gx % 2 == 0
    held, rows, cols = own_ref.shape
    fields, species = loadings_ref.shape
    per_row = LANES // species
    sums = fields // per_row
    for r in range(sums):
        total = jnp.sum(blocks_ref[:, r, :, :], axis=0) * scale
        for q in range(per_row):
            loadings_ref[q * sums + r:q * sums + r + 1, :] = total[:, q * species:(q + 1) * species]

    rim = held * rows
    north, south = jnp.maximum(gx - 1, 0), jnp.minimum(gx + 1, down_count - 1)
    has_north = jnp.where(gx > 0, 1.0, 0.0)
    has_south = jnp.where(gx < down_count - 1, 1.0, 0.0)
    lane = iota((1, LANES), 1)

    def column(j, present):
        middle, upper, lower = blocks_ref[gx * across + j, sums], blocks_ref[north * across + j, sums], blocks_ref[south * across + j, sums]
        first, last = lane % rows == 0, lane % rows == rows - 1
        corners = jnp.where(first, pltpu.roll(upper, LANES - (rows - 1), 1), 0.0) * has_north
        corners = corners + jnp.where(last, pltpu.roll(lower, rows - 1, 1), 0.0) * has_south
        corners = jnp.where(lane < rim, corners, 0.0)
        once = pltpu.roll(middle, LANES - rim, 1) - corners
        return [row_to_column(row * present, rim, 0) for row in (middle, once, corners)]

    west = column(jnp.maximum(gy - 1, 0), jnp.where(gy > 0, 1.0, 0.0))
    east = column(jnp.minimum(gy + 1, across - 1), jnp.where(gy < across - 1, 1.0, 0.0))
    row, col = iota((rows, LANES), 0), iota((rows, LANES), 1)

    def addition(k, columns, at, own, kappa, edge, inner, present):
        field, once, corners = [value[k * rows:(k + 1) * rows] for value in columns]
        once = once - own * present
        field = jnp.broadcast_to(field, (rows, LANES))
        beside = jnp.where(row == 0, 0.0, pltpu.roll(field, 1, 0)) + jnp.where(row == rows - 1, 0.0, pltpu.roll(field, rows - 1, 0))
        outer = beside - (kappa + 4.0) * field - once + corners
        return jnp.where(col == edge, outer, 0.0) + jnp.where(col == inner, field, 0.0)

    for k in range(held):
        own, kappa = own_ref[k], kappa_ref[k]
        above_edge = jnp.where(is_even, odd_ref[k], even_ref[k])
        below_edge = jnp.where(is_even, even_ref[k], odd_ref[k])
        once = operator(own, kappa, above_edge[:1], below_edge[:1], 0.0, 0.0)
        above = (above_edge[1:] - own[:1]) * has_north
        below = (below_edge[1:] - own[rows - 1:]) * has_south
        rest_ref[k] = mine_ref[k] - operator(once, kappa, above, below, 0.0, 0.0)
        span = slice(0, LANES)
        rest_ref[k, :, span] -= addition(
            k, west, span, own_ref[k, :, :1], kappa_ref[k, :, span], 0, 1, jnp.where(gy > 0, 1.0, 0.0))
        span = slice(cols - LANES, cols)
        rest_ref[k, :, span] -= addition(
            k, east, span, own_ref[k, :, cols - 1:], kappa_ref[k, :, span], LANES - 1, LANES - 2, jnp.where(gy < across - 1, 1.0, 0.0))


def final_kernel(rest_ref, other_ref, latent_ref):
    latent_ref[...] = rest_ref[...] + other_ref[...]


def per_device(latent, kappa_sq, coefs, loadings, counts, land):
    fields, rows, cols = latent.shape
    species = loadings.shape[0]
    held = kappa_sq.shape[0]
    down_count, across, groups = lax.axis_size("gx"), lax.axis_size("gy"), lax.axis_size("sp")
    peers = down_count * across
    lines = fields * species // LANES + 1
    f32 = jnp.float32
    field_block = jax.ShapeDtypeStruct((held, rows, cols), f32)
    edge_block = jax.ShapeDtypeStruct((held, 2, cols), f32)
    vmem = pl.BlockSpec(memory_space=pltpu.VMEM)
    hbm = pl.BlockSpec(memory_space=pltpu.HBM)
    pieces = rows // TILE * SPLIT
    half_block = jax.ShapeDtypeStruct((groups // 2, held, rows, cols), f32)
    blocks, own, odd_edge, even_edge, sent, kept = pl.pallas_call(
        functools.partial(local_kernel, peers, across),
        in_specs=[hbm] * 6,
        out_specs=[vmem] * 6,
        out_shape=[
            jax.ShapeDtypeStruct((peers, lines, 1, LANES), f32), field_block, edge_block, edge_block, half_block, half_block,
        ],
        scratch_shapes=[
            pltpu.VMEM(latent.shape, f32),
            pltpu.VMEM((fields, species), f32),
            pltpu.VMEM(latent.shape, f32),
            pltpu.VMEM(kappa_sq.shape, f32),
            pltpu.VMEM(coefs.shape, f32),
            pltpu.VMEM(counts.shape, jnp.int32),
            pltpu.VMEM(land.shape, jnp.int32),
            pltpu.SemaphoreType.DMA((3 * pieces + 3,)),
        ],
        compiler_params=pltpu.CompilerParams(vmem_limit_bytes=60 * 2**20),
    )(loadings.T, latent, kappa_sq, coefs, counts, land)
    blocks = lax.all_to_all(blocks, ("gx", "gy"), 0, 0, tiled=True)

    def exchanged(edge, first):
        pairs = [(i, i + 1) for i in range(first, down_count - 1, 2)]
        return lax.ppermute(edge, "gx", pairs + [(j, i) for i, j in pairs])

    by_odd, by_even = exchanged(odd_edge, 1), exchanged(even_edge, 0)
    params = pltpu.CompilerParams(vmem_limit_bytes=16 * 2**20)
    received = lax.ppermute(sent, "sp", [(i, i ^ NEAR) for i in range(groups)])
    mine, sent = pl.pallas_call(
        add_kernel,
        in_specs=[vmem] * 2,
        out_specs=[vmem] * 2,
        out_shape=[field_block] * 2,
        compiler_params=params,
        cost_estimate=pl.CostEstimate(flops=10**6, bytes_accessed=2**20, transcendentals=0),
    )(kept, received)
    other = lax.ppermute(sent, "sp", [(i, i ^ FAR) for i in range(groups)])
    scale = 1.0 / math.sqrt(rows * down_count * cols * across)
    rest, grad_loadings = pl.pallas_call(
        functools.partial(prior_kernel, scale, down_count, across),
        in_specs=[vmem] * 6,
        out_specs=[vmem] * 2,
        out_shape=[field_block, jax.ShapeDtypeStruct((fields, species), f32)],
        compiler_params=params,
        cost_estimate=pl.CostEstimate(flops=3*10**9, bytes_accessed=2**20, transcendentals=0),
    )(blocks, own, kappa_sq, mine, by_odd, by_even)
    grad_latent = pl.pallas_call(
        final_kernel,
        in_specs=[vmem] * 2,
        out_specs=vmem,
        out_shape=field_block,
        compiler_params=params,
    )(rest, other)
    return grad_latent, grad_loadings.T


def solution(mesh):
    return jax.shard_map(
        per_device,
        mesh=mesh,
        in_specs=(
            P(None, "gx", "gy"),
            P("sp", "gx", "gy"),
            P("sp", "gx", "gy"),
            P("sp", None),
            P("sp", "gx", "gy"),
            P("gx", "gy"),
        ),
        out_specs=(P("sp", "gx", "gy"), P("sp", None)),
        check_vma=False,
    )
```

```python
import functools
import math

import jax
import jax.numpy as jnp
from jax import lax
from jax.experimental import pallas as pl
from jax.experimental.pallas import tpu as pltpu
from jax.sharding import PartitionSpec as P

HIGHEST = lax.Precision.HIGHEST
TILE = 8
LANES = 128
SPLIT = 1
NEAR, FAR = 1, 3


def iota(shape, dim):
    return lax.broadcasted_iota(jnp.int32, shape, dim)


def dot(a, b, contract):
    return lax.dot_general(a, b, (contract, ((), ())), precision=HIGHEST, preferred_element_type=jnp.float32)


def operator(field, kappa, above, below, left, right):
    rows, cols = field.shape
    row, col = iota(field.shape, 0), iota(field.shape, 1)
    up = jnp.where(row == 0, above, pltpu.roll(field, 1, 0))
    down = jnp.where(row == rows - 1, below, pltpu.roll(field, rows - 1, 0))
    west = jnp.where(col == 0, left, pltpu.roll(field, 1, 1))
    east = jnp.where(col == cols - 1, right, pltpu.roll(field, cols - 1, 1))
    return (kappa + 4.0) * field - ((down + up) + (east + west))


def column_to_row(column, offset):
    shape = (column.shape[0], LANES)
    placed = jnp.where(iota(shape, 1) == iota(shape, 0) + offset, column, 0.0)
    return jnp.sum(placed, axis=0, keepdims=True)


def row_to_column(row, count, offset):
    shape = (count, LANES)
    placed = jnp.where(iota(shape, 1) == iota(shape, 0) + offset, row, 0.0)
    return jnp.sum(placed, axis=1, keepdims=True)


def parts_of(value, count):
    parts = []
    for _ in range(count):
        part = value.astype(jnp.bfloat16)
        parts.append(part)
        value = value - part.astype(jnp.float32)
    return parts


def spread_of(rows, cols, dim):
    one, many = iota((rows, cols), dim), iota((rows, cols), 1 - dim)
    return jnp.where(many // TILE == one, 1.0, 0.0)


def on_diagonal(value):
    return jnp.where(iota(value.shape, 0) % TILE == iota(value.shape, 1) % TILE, value, 0.0)


def bf16_dot(a, b, contract):
    return lax.dot_general(a, b, (contract, ((), ())), preferred_element_type=jnp.float32)


def local_kernel(
    peers, across,
    loadings_hbm, latent_hbm, kappa_hbm, coefs_hbm, counts_hbm, land_hbm,
    blocks_ref, own_ref, odd_ref, even_ref, sent_ref, kept_ref,
    species_ref, loadings_ref, latent_ref, kappa_ref, coefs_ref, counts_ref, land_ref, sems,
):
    fields, species = loadings_ref.shape
    held, rows, cols = kappa_ref.shape
    sp, gy = lax.axis_index("sp"), lax.axis_index("gy")
    flat_fields, flat_species = fields * TILE, species * TILE
    width = cols // SPLIT
    pieces = [(r, c) for r in range(rows // TILE) for c in range(SPLIT)]
    copies = []
    for n, (r, c) in enumerate(pieces):
        at = (slice(None), pl.ds(r * TILE, TILE), pl.ds(c * width, width))
        pairs = [(latent_hbm, latent_ref), (coefs_hbm, coefs_ref), (counts_hbm, counts_ref)]
        copies.append([
            pltpu.make_async_copy(source.at[at], target.at[at], sems.at[3 * n + i])
            for i, (source, target) in enumerate(pairs)
        ])
    whole = 3 * len(pieces)
    loadings_copy = pltpu.make_async_copy(loadings_hbm, loadings_ref, sems.at[whole])
    land_copy = pltpu.make_async_copy(land_hbm, land_ref, sems.at[whole + 1])
    kappa_copy = pltpu.make_async_copy(kappa_hbm, kappa_ref, sems.at[whole + 2])
    latents = [piece[0] for piece in copies]
    others = [copy for piece in copies for copy in piece[1:]]
    for copy in [loadings_copy, *latents, kappa_copy, land_copy, *others]:
        copy.start()

    loadings_copy.wait()
    transposed = loadings_ref[...]
    wide = dot(transposed, spread_of(fields, flat_fields, 0), ((0,), (0,)))
    wide = jnp.broadcast_to(wide[:, None, :], (species, TILE, flat_fields)).reshape(flat_species, flat_fields)
    wide = parts_of(on_diagonal(wide), 3)
    wide = jnp.concatenate([wide[0], wide[0], wide[0], wide[1], wide[1], wide[2]], axis=1)
    tall = dot(transposed, spread_of(species, flat_species, 0), ((1,), (0,)))
    tall = jnp.broadcast_to(tall[:, None, :], (fields, TILE, flat_species)).reshape(flat_fields, flat_species)
    tall = parts_of(on_diagonal(tall), 2)
    tall = jnp.concatenate([tall[0], tall[0], tall[1]], axis=1)

    spans = [(slice(None), slice(r * TILE, (r + 1) * TILE), slice(c * width, (c + 1) * width)) for r, c in pieces]
    latents, mixes = [], []
    for n, at in enumerate(spans):
        copies[n][0].wait()
        latent = parts_of(latent_ref[at].reshape(flat_fields, width), 3)
        stacked = jnp.concatenate([latent[0], latent[1], latent[2], latent[0], latent[1], latent[0]], axis=0)
        mixes.append(bf16_dot(wide, stacked, ((1,), (0,))))
        latents.append(latent)
    land_copy.wait()
    gram = None
    for n, at in enumerate(spans):
        copies[n][1].wait()
        copies[n][2].wait()
        rate = jnp.exp(coefs_ref[at].reshape(flat_species, width) + mixes[n])
        counts = counts_ref[at].reshape(flat_species, width).astype(jnp.float32)
        land = jnp.broadcast_to(land_ref[at[1:]].astype(jnp.float32)[None], (species, TILE, width))
        resid = parts_of(land.reshape(flat_species, width) * (counts - rate), 2)
        latent = latents[n]
        both = bf16_dot(resid[0], jnp.concatenate([latent[0], latent[1]], axis=0), ((1,), (1,)))
        partial = both[:, :flat_fields] + both[:, flat_fields:] + bf16_dot(resid[1], latent[0], ((1,), (1,)))
        gram = partial if gram is None else gram + partial
        stacked = jnp.concatenate([resid[0], resid[1], resid[0]], axis=0)
        species_ref[at] = bf16_dot(tall, stacked, ((1,), (0,))).reshape(fields, TILE, width)

    kappa_copy.wait()
    first = sp * held
    is_even = lax.axis_index("gx") % 2 == 0
    own_ref[...] = latent_ref[pl.ds(first, held)]
    rim = rows * held
    west, east = jnp.zeros((1, LANES), jnp.float32), jnp.zeros((1, LANES), jnp.float32)
    for k in range(held):
        own = latent_ref[first + k]
        once = operator(own, kappa_ref[k], 0.0, 0.0, 0.0, 0.0)
        head = jnp.concatenate([own[:1], once[:1]], axis=0)
        tail = jnp.concatenate([own[-1:], once[-1:]], axis=0)
        odd_ref[k] = jnp.where(is_even, head, tail)
        even_ref[k] = jnp.where(is_even, tail, head)
        west = west + column_to_row(own[:, :1], k * rows) + column_to_row(once[:, :1], rim + k * rows)
        east = east + column_to_row(own[:, cols - 1:], k * rows) + column_to_row(once[:, cols - 1:], rim + k * rows)
    for ref, owners in ((kept_ref, (sp, sp ^ FAR)), (sent_ref, (sp ^ NEAR, sp ^ NEAR ^ FAR))):
        for half, owner in enumerate(owners):
            ref[half] = species_ref[pl.ds(owner * held, held)]
    total = jnp.sum(on_diagonal(gram).reshape(species, TILE, flat_fields), axis=1)
    total = dot(spread_of(fields, flat_fields, 0), total, ((1,), (1,)))
    per_row = LANES // species
    sums = fields // per_row
    packed = jnp.concatenate([total[q * sums:(q + 1) * sums] for q in range(per_row)], axis=1)
    for peer in range(peers):
        blocks_ref[peer, :sums] = packed[:, None, :]
        blocks_ref[peer, sums] = jnp.where(peer % across < gy, west, east)


def add_kernel(kept_ref, received_ref, mine_ref, sent_ref):
    mine_ref[...] = kept_ref[0] + received_ref[0]
    sent_ref[...] = kept_ref[1] + received_ref[1]


def prior_kernel(
    scale, down_count, across, blocks_ref, own_ref, kappa_ref, mine_ref, odd_ref, even_ref, rest_ref, loadings_ref,
):
    gy, gx = lax.axis_index("gy"), lax.axis_index("gx")
    is_even = gx % 2 == 0
    held, rows, cols = own_ref.shape
    fields, species = loadings_ref.shape
    per_row = LANES // species
    sums = fields // per_row
    for r in range(sums):
        total = jnp.sum(blocks_ref[:, r, :, :], axis=0) * scale
        for q in range(per_row):
            loadings_ref[q * sums + r:q * sums + r + 1, :] = total[:, q * species:(q + 1) * species]

    rim = held * rows
    north, south = jnp.maximum(gx - 1, 0), jnp.minimum(gx + 1, down_count - 1)
    has_north = jnp.where(gx > 0, 1.0, 0.0)
    has_south = jnp.where(gx < down_count - 1, 1.0, 0.0)
    lane = iota((1, LANES), 1)

    def column(j, present):
        middle, upper, lower = blocks_ref[gx * across + j, sums], blocks_ref[north * across + j, sums], blocks_ref[south * across + j, sums]
        first, last = lane % rows == 0, lane % rows == rows - 1
        corners = jnp.where(first, pltpu.roll(upper, LANES - (rows - 1), 1), 0.0) * has_north
        corners = corners + jnp.where(last, pltpu.roll(lower, rows - 1, 1), 0.0) * has_south
        corners = jnp.where(lane < rim, corners, 0.0)
        once = pltpu.roll(middle, LANES - rim, 1) - corners
        return [row_to_column(row * present, rim, 0) for row in (middle, once, corners)]

    west = column(jnp.maximum(gy - 1, 0), jnp.where(gy > 0, 1.0, 0.0))
    east = column(jnp.minimum(gy + 1, across - 1), jnp.where(gy < across - 1, 1.0, 0.0))
    row, col = iota((rows, LANES), 0), iota((rows, LANES), 1)

    def addition(k, columns, at, own, kappa, edge, inner, present):
        field, once, corners = [value[k * rows:(k + 1) * rows] for value in columns]
        once = once - own * present
        field = jnp.broadcast_to(field, (rows, LANES))
        beside = jnp.where(row == 0, 0.0, pltpu.roll(field, 1, 0)) + jnp.where(row == rows - 1, 0.0, pltpu.roll(field, rows - 1, 0))
        outer = beside - (kappa + 4.0) * field - once + corners
        return jnp.where(col == edge, outer, 0.0) + jnp.where(col == inner, field, 0.0)

    for k in range(held):
        own, kappa = own_ref[k], kappa_ref[k]
        above_edge = jnp.where(is_even, odd_ref[k], even_ref[k])
        below_edge = jnp.where(is_even, even_ref[k], odd_ref[k])
        once = operator(own, kappa, above_edge[:1], below_edge[:1], 0.0, 0.0)
        above = (above_edge[1:] - own[:1]) * has_north
        below = (below_edge[1:] - own[rows - 1:]) * has_south
        rest_ref[k] = mine_ref[k] - operator(once, kappa, above, below, 0.0, 0.0)
        span = slice(0, LANES)
        rest_ref[k, :, span] -= addition(
            k, west, span, own_ref[k, :, :1], kappa_ref[k, :, span], 0, 1, jnp.where(gy > 0, 1.0, 0.0))
        span = slice(cols - LANES, cols)
        rest_ref[k, :, span] -= addition(
            k, east, span, own_ref[k, :, cols - 1:], kappa_ref[k, :, span], LANES - 1, LANES - 2, jnp.where(gy < across - 1, 1.0, 0.0))


def per_device(latent, kappa_sq, coefs, loadings, counts, land):
    fields, rows, cols = latent.shape
    species = loadings.shape[0]
    held = kappa_sq.shape[0]
    down_count, across, groups = lax.axis_size("gx"), lax.axis_size("gy"), lax.axis_size("sp")
    peers = down_count * across
    lines = fields * species // LANES + 1
    f32 = jnp.float32
    field_block = jax.ShapeDtypeStruct((held, rows, cols), f32)
    edge_block = jax.ShapeDtypeStruct((held, 2, cols), f32)
    vmem = pl.BlockSpec(memory_space=pltpu.VMEM)
    hbm = pl.BlockSpec(memory_space=pltpu.HBM)
    pieces = rows // TILE * SPLIT
    half_block = jax.ShapeDtypeStruct((groups // 2, held, rows, cols), f32)
    blocks, own, odd_edge, even_edge, sent, kept = pl.pallas_call(
        functools.partial(local_kernel, peers, across),
        in_specs=[hbm] * 6,
        out_specs=[vmem] * 6,
        out_shape=[
            jax.ShapeDtypeStruct((peers, lines, 1, LANES), f32), field_block, edge_block, edge_block, half_block, half_block,
        ],
        scratch_shapes=[
            pltpu.VMEM(latent.shape, f32),
            pltpu.VMEM((fields, species), f32),
            pltpu.VMEM(latent.shape, f32),
            pltpu.VMEM(kappa_sq.shape, f32),
            pltpu.VMEM(coefs.shape, f32),
            pltpu.VMEM(counts.shape, jnp.int32),
            pltpu.VMEM(land.shape, jnp.int32),
            pltpu.SemaphoreType.DMA((3 * pieces + 3,)),
        ],
        compiler_params=pltpu.CompilerParams(vmem_limit_bytes=60 * 2**20),
    )(loadings.T, latent, kappa_sq, coefs, counts, land)
    blocks = lax.all_to_all(blocks, ("gx", "gy"), 0, 0, tiled=True)

    def exchanged(edge, first):
        pairs = [(i, i + 1) for i in range(first, down_count - 1, 2)]
        return lax.ppermute(edge, "gx", pairs + [(j, i) for i, j in pairs])

    by_odd, by_even = exchanged(odd_edge, 1), exchanged(even_edge, 0)
    params = pltpu.CompilerParams(vmem_limit_bytes=16 * 2**20)
    received = lax.ppermute(sent, "sp", [(i, i ^ NEAR) for i in range(groups)])
    mine, sent = pl.pallas_call(
        add_kernel,
        in_specs=[vmem] * 2,
        out_specs=[vmem] * 2,
        out_shape=[field_block] * 2,
        compiler_params=params,
        cost_estimate=pl.CostEstimate(flops=10**6, bytes_accessed=2**20, transcendentals=0),
    )(kept, received)
    other = lax.ppermute(sent, "sp", [(i, i ^ FAR) for i in range(groups)])
    scale = 1.0 / math.sqrt(rows * down_count * cols * across)
    rest, grad_loadings = pl.pallas_call(
        functools.partial(prior_kernel, scale, down_count, across),
        in_specs=[vmem] * 6,
        out_specs=[vmem] * 2,
        out_shape=[field_block, jax.ShapeDtypeStruct((fields, species), f32)],
        compiler_params=params,
        cost_estimate=pl.CostEstimate(flops=3*10**9, bytes_accessed=2**20, transcendentals=0),
    )(blocks, own, kappa_sq, mine, by_odd, by_even)
    return rest + other, grad_loadings.T


def solution(mesh):
    return jax.shard_map(
        per_device,
        mesh=mesh,
        in_specs=(
            P(None, "gx", "gy"),
            P("sp", "gx", "gy"),
            P("sp", "gx", "gy"),
            P("sp", None),
            P("sp", "gx", "gy"),
            P("gx", "gy"),
        ),
        out_specs=(P("sp", "gx", "gy"), P("sp", None)),
        check_vma=False,
    )
```

```python
import functools
import math

import jax
import jax.numpy as jnp
from jax import lax
from jax.experimental import pallas as pl
from jax.experimental.pallas import tpu as pltpu
from jax.sharding import PartitionSpec as P

HIGHEST = lax.Precision.HIGHEST
TILE = 8
LANES = 128
SPLIT = 1
NEAR, FAR = 1, 3


def iota(shape, dim):
    return lax.broadcasted_iota(jnp.int32, shape, dim)


def dot(a, b, contract):
    return lax.dot_general(a, b, (contract, ((), ())), precision=HIGHEST, preferred_element_type=jnp.float32)


def operator(field, kappa, above, below, left, right):
    rows, cols = field.shape
    row, col = iota(field.shape, 0), iota(field.shape, 1)
    up = jnp.where(row == 0, above, pltpu.roll(field, 1, 0))
    down = jnp.where(row == rows - 1, below, pltpu.roll(field, rows - 1, 0))
    west = jnp.where(col == 0, left, pltpu.roll(field, 1, 1))
    east = jnp.where(col == cols - 1, right, pltpu.roll(field, cols - 1, 1))
    return (kappa + 4.0) * field - ((down + up) + (east + west))


def column_to_row(column, offset):
    shape = (column.shape[0], LANES)
    placed = jnp.where(iota(shape, 1) == iota(shape, 0) + offset, column, 0.0)
    return jnp.sum(placed, axis=0, keepdims=True)


def row_to_column(row, count, offset):
    shape = (count, LANES)
    placed = jnp.where(iota(shape, 1) == iota(shape, 0) + offset, row, 0.0)
    return jnp.sum(placed, axis=1, keepdims=True)


def parts_of(value, count):
    parts = []
    for _ in range(count):
        part = value.astype(jnp.bfloat16)
        parts.append(part)
        value = value - part.astype(jnp.float32)
    return parts


def spread_of(rows, cols, dim):
    one, many = iota((rows, cols), dim), iota((rows, cols), 1 - dim)
    return jnp.where(many // TILE == one, 1.0, 0.0)


def on_diagonal(value):
    return jnp.where(iota(value.shape, 0) % TILE == iota(value.shape, 1) % TILE, value, 0.0)


def bf16_dot(a, b, contract):
    return lax.dot_general(a, b, (contract, ((), ())), preferred_element_type=jnp.float32)


def local_kernel(
    peers, across,
    loadings_hbm, latent_hbm, kappa_hbm, coefs_hbm, counts_hbm, land_hbm,
    blocks_ref, own_ref, odd_ref, even_ref, sent_ref, kept_ref,
    species_ref, loadings_ref, latent_ref, kappa_ref, coefs_ref, counts_ref, land_ref, sems,
):
    fields, species = loadings_ref.shape
    held, rows, cols = kappa_ref.shape
    sp, gy = lax.axis_index("sp"), lax.axis_index("gy")
    flat_fields, flat_species = fields * TILE, species * TILE
    width = cols // SPLIT
    pieces = [(r, c) for r in range(rows // TILE) for c in range(SPLIT)]
    copies = []
    for n, (r, c) in enumerate(pieces):
        at = (slice(None), pl.ds(r * TILE, TILE), pl.ds(c * width, width))
        pairs = [(latent_hbm, latent_ref), (coefs_hbm, coefs_ref), (counts_hbm, counts_ref)]
        copies.append([
            pltpu.make_async_copy(source.at[at], target.at[at], sems.at[3 * n + i])
            for i, (source, target) in enumerate(pairs)
        ])
    whole = 3 * len(pieces)
    loadings_copy = pltpu.make_async_copy(loadings_hbm, loadings_ref, sems.at[whole])
    land_copy = pltpu.make_async_copy(land_hbm, land_ref, sems.at[whole + 1])
    kappa_copy = pltpu.make_async_copy(kappa_hbm, kappa_ref, sems.at[whole + 2])
    latents = [piece[0] for piece in copies]
    others = [copy for piece in copies for copy in piece[1:]]
    for copy in [loadings_copy, *latents, kappa_copy, land_copy, *others]:
        copy.start()

    loadings_copy.wait()
    transposed = loadings_ref[...]
    wide = dot(transposed, spread_of(fields, flat_fields, 0), ((0,), (0,)))
    wide = jnp.broadcast_to(wide[:, None, :], (species, TILE, flat_fields)).reshape(flat_species, flat_fields)
    wide = parts_of(on_diagonal(wide), 3)
    wide = jnp.concatenate([wide[0], wide[0], wide[0], wide[1], wide[1], wide[2]], axis=1)
    tall = dot(transposed, spread_of(species, flat_species, 0), ((1,), (0,)))
    tall = jnp.broadcast_to(tall[:, None, :], (fields, TILE, flat_species)).reshape(flat_fields, flat_species)
    tall = parts_of(on_diagonal(tall), 2)
    tall = jnp.concatenate([tall[0], tall[0], tall[1]], axis=1)

    spans = [(slice(None), slice(r * TILE, (r + 1) * TILE), slice(c * width, (c + 1) * width)) for r, c in pieces]
    latents, mixes = [], []
    for n, at in enumerate(spans):
        copies[n][0].wait()
        latent = parts_of(latent_ref[at].reshape(flat_fields, width), 3)
        stacked = jnp.concatenate([latent[0], latent[1], latent[2], latent[0], latent[1], latent[0]], axis=0)
        mixes.append(bf16_dot(wide, stacked, ((1,), (0,))))
        latents.append(latent)
    land_copy.wait()
    gram = None
    for n, at in enumerate(spans):
        copies[n][1].wait()
        copies[n][2].wait()
        rate = jnp.exp(coefs_ref[at].reshape(flat_species, width) + mixes[n])
        counts = counts_ref[at].reshape(flat_species, width).astype(jnp.float32)
        land = jnp.broadcast_to(land_ref[at[1:]].astype(jnp.float32)[None], (species, TILE, width))
        resid = parts_of(land.reshape(flat_species, width) * (counts - rate), 2)
        latent = latents[n]
        both = bf16_dot(resid[0], jnp.concatenate([latent[0], latent[1]], axis=0), ((1,), (1,)))
        partial = both[:, :flat_fields] + both[:, flat_fields:] + bf16_dot(resid[1], latent[0], ((1,), (1,)))
        gram = partial if gram is None else gram + partial
        stacked = jnp.concatenate([resid[0], resid[1], resid[0]], axis=0)
        species_ref[at] = bf16_dot(tall, stacked, ((1,), (0,))).reshape(fields, TILE, width)

    kappa_copy.wait()
    first = sp * held
    is_even = lax.axis_index("gx") % 2 == 0
    own_ref[...] = latent_ref[pl.ds(first, held)]
    rim = rows * held
    west, east = jnp.zeros((1, LANES), jnp.float32), jnp.zeros((1, LANES), jnp.float32)
    for k in range(held):
        own = latent_ref[first + k]
        once = operator(own, kappa_ref[k], 0.0, 0.0, 0.0, 0.0)
        head = jnp.concatenate([own[:1], once[:1]], axis=0)
        tail = jnp.concatenate([own[-1:], once[-1:]], axis=0)
        odd_ref[k] = jnp.where(is_even, head, tail)
        even_ref[k] = jnp.where(is_even, tail, head)
        west = west + column_to_row(own[:, :1], k * rows) + column_to_row(once[:, :1], rim + k * rows)
        east = east + column_to_row(own[:, cols - 1:], k * rows) + column_to_row(once[:, cols - 1:], rim + k * rows)
    for ref, owners in ((kept_ref, (sp, sp ^ FAR)), (sent_ref, (sp ^ NEAR, sp ^ NEAR ^ FAR))):
        for half, owner in enumerate(owners):
            ref[half] = species_ref[pl.ds(owner * held, held)]
    total = jnp.sum(on_diagonal(gram).reshape(species, TILE, flat_fields), axis=1)
    total = dot(spread_of(fields, flat_fields, 0), total, ((1,), (1,)))
    per_row = LANES // species
    sums = fields // per_row
    packed = jnp.concatenate([total[q * sums:(q + 1) * sums] for q in range(per_row)], axis=1)
    for peer in range(peers):
        blocks_ref[peer, :sums] = packed[:, None, :]
        blocks_ref[peer, sums] = jnp.where(peer % across < gy, west, east)


def add_kernel(kept_ref, received_ref, mine_ref, sent_ref):
    mine_ref[...] = kept_ref[0] + received_ref[0]
    sent_ref[...] = kept_ref[1] + received_ref[1]


def prior_kernel(
    scale, down_count, across, blocks_ref, own_ref, kappa_ref, mine_ref, even_ref, odd_ref, rest_ref, loadings_ref,
):
    gy, gx = lax.axis_index("gy"), lax.axis_index("gx")
    is_even = gx % 2 == 0
    held, rows, cols = own_ref.shape
    fields, species = loadings_ref.shape
    per_row = LANES // species
    sums = fields // per_row
    for r in range(sums):
        total = jnp.sum(blocks_ref[:, r, :, :], axis=0) * scale
        for q in range(per_row):
            loadings_ref[q * sums + r:q * sums + r + 1, :] = total[:, q * species:(q + 1) * species]

    rim = held * rows
    north, south = jnp.maximum(gx - 1, 0), jnp.minimum(gx + 1, down_count - 1)
    has_north = jnp.where(gx > 0, 1.0, 0.0)
    has_south = jnp.where(gx < down_count - 1, 1.0, 0.0)
    lane = iota((1, LANES), 1)

    def column(j, present):
        middle, upper, lower = blocks_ref[gx * across + j, sums], blocks_ref[north * across + j, sums], blocks_ref[south * across + j, sums]
        first, last = lane % rows == 0, lane % rows == rows - 1
        corners = jnp.where(first, pltpu.roll(upper, LANES - (rows - 1), 1), 0.0) * has_north
        corners = corners + jnp.where(last, pltpu.roll(lower, rows - 1, 1), 0.0) * has_south
        corners = jnp.where(lane < rim, corners, 0.0)
        once = pltpu.roll(middle, LANES - rim, 1) - corners
        return [row_to_column(row * present, rim, 0) for row in (middle, once, corners)]

    west = column(jnp.maximum(gy - 1, 0), jnp.where(gy > 0, 1.0, 0.0))
    east = column(jnp.minimum(gy + 1, across - 1), jnp.where(gy < across - 1, 1.0, 0.0))
    row, col = iota((rows, LANES), 0), iota((rows, LANES), 1)

    def addition(k, columns, at, own, kappa, edge, inner, present):
        field, once, corners = [value[k * rows:(k + 1) * rows] for value in columns]
        once = once - own * present
        field = jnp.broadcast_to(field, (rows, LANES))
        beside = jnp.where(row == 0, 0.0, pltpu.roll(field, 1, 0)) + jnp.where(row == rows - 1, 0.0, pltpu.roll(field, rows - 1, 0))
        outer = beside - (kappa + 4.0) * field - once + corners
        return jnp.where(col == edge, outer, 0.0) + jnp.where(col == inner, field, 0.0)

    for k in range(held):
        own, kappa = own_ref[k], kappa_ref[k]
        above_edge = jnp.where(is_even, odd_ref[k], even_ref[k])
        below_edge = jnp.where(is_even, even_ref[k], odd_ref[k])
        once = operator(own, kappa, above_edge[:1], below_edge[:1], 0.0, 0.0)
        above = (above_edge[1:] - own[:1]) * has_north
        below = (below_edge[1:] - own[rows - 1:]) * has_south
        rest_ref[k] = mine_ref[k] - operator(once, kappa, above, below, 0.0, 0.0)
        span = slice(0, LANES)
        rest_ref[k, :, span] -= addition(
            k, west, span, own_ref[k, :, :1], kappa_ref[k, :, span], 0, 1, jnp.where(gy > 0, 1.0, 0.0))
        span = slice(cols - LANES, cols)
        rest_ref[k, :, span] -= addition(
            k, east, span, own_ref[k, :, cols - 1:], kappa_ref[k, :, span], LANES - 1, LANES - 2, jnp.where(gy < across - 1, 1.0, 0.0))


def per_device(latent, kappa_sq, coefs, loadings, counts, land):
    fields, rows, cols = latent.shape
    species = loadings.shape[0]
    held = kappa_sq.shape[0]
    down_count, across, groups = lax.axis_size("gx"), lax.axis_size("gy"), lax.axis_size("sp")
    peers = down_count * across
    lines = fields * species // LANES + 1
    f32 = jnp.float32
    field_block = jax.ShapeDtypeStruct((held, rows, cols), f32)
    edge_block = jax.ShapeDtypeStruct((held, 2, cols), f32)
    vmem = pl.BlockSpec(memory_space=pltpu.VMEM)
    hbm = pl.BlockSpec(memory_space=pltpu.HBM)
    pieces = rows // TILE * SPLIT
    half_block = jax.ShapeDtypeStruct((groups // 2, held, rows, cols), f32)
    blocks, own, odd_edge, even_edge, sent, kept = pl.pallas_call(
        functools.partial(local_kernel, peers, across),
        in_specs=[hbm] * 6,
        out_specs=[vmem] * 6,
        out_shape=[
            jax.ShapeDtypeStruct((peers, lines, 1, LANES), f32), field_block, edge_block, edge_block, half_block, half_block,
        ],
        scratch_shapes=[
            pltpu.VMEM(latent.shape, f32),
            pltpu.VMEM((fields, species), f32),
            pltpu.VMEM(latent.shape, f32),
            pltpu.VMEM(kappa_sq.shape, f32),
            pltpu.VMEM(coefs.shape, f32),
            pltpu.VMEM(counts.shape, jnp.int32),
            pltpu.VMEM(land.shape, jnp.int32),
            pltpu.SemaphoreType.DMA((3 * pieces + 3,)),
        ],
        compiler_params=pltpu.CompilerParams(vmem_limit_bytes=60 * 2**20),
    )(loadings.T, latent, kappa_sq, coefs, counts, land)
    blocks = lax.all_to_all(blocks, ("gx", "gy"), 0, 0, tiled=True)

    def exchanged(edge, first):
        pairs = [(i, i + 1) for i in range(first, down_count - 1, 2)]
        return lax.ppermute(edge, "gx", pairs + [(j, i) for i, j in pairs])

    by_odd, by_even = exchanged(odd_edge, 1), exchanged(even_edge, 0)
    params = pltpu.CompilerParams(vmem_limit_bytes=16 * 2**20)
    received = lax.ppermute(sent, "sp", [(i, i ^ NEAR) for i in range(groups)])
    mine, sent = pl.pallas_call(
        add_kernel,
        in_specs=[vmem] * 2,
        out_specs=[vmem] * 2,
        out_shape=[field_block] * 2,
        compiler_params=params,
        cost_estimate=pl.CostEstimate(flops=10**6, bytes_accessed=2**20, transcendentals=0),
    )(kept, received)
    other = lax.ppermute(sent, "sp", [(i, i ^ FAR) for i in range(groups)])
    scale = 1.0 / math.sqrt(rows * down_count * cols * across)
    rest, grad_loadings = pl.pallas_call(
        functools.partial(prior_kernel, scale, down_count, across),
        in_specs=[vmem] * 6,
        out_specs=[vmem] * 2,
        out_shape=[field_block, jax.ShapeDtypeStruct((fields, species), f32)],
        compiler_params=params,
        cost_estimate=pl.CostEstimate(flops=3*10**9, bytes_accessed=2**20, transcendentals=0),
    )(blocks, own, kappa_sq, mine, by_even, by_odd)
    return rest + other, grad_loadings.T


def solution(mesh):
    return jax.shard_map(
        per_device,
        mesh=mesh,
        in_specs=(
            P(None, "gx", "gy"),
            P("sp", "gx", "gy"),
            P("sp", "gx", "gy"),
            P("sp", None),
            P("sp", "gx", "gy"),
            P("gx", "gy"),
        ),
        out_specs=(P("sp", "gx", "gy"), P("sp", None)),
        check_vma=False,
    )
```
